512 devices in a mesh: dp: 128 (over z, x, y_lo), sub: 4 (over y_hi, core).
Axes of the slice: x: 4, y: 4 (y_hi: 2, y_lo: 2; y = y_hi * 2 + y_lo), z: 16, core: 2. Of those that a mesh axis runs over, the one named last changes fastest.
Arguments:
- queries: bfloat16 [16384, 4096], P('dp', 'sub'), may hold values from -1 to 1
- passages: bfloat16 [768, 4096], P('dp', 'sub'), may hold values from -1 to 1
- positive_bank: bfloat16 [2048, 4096], P('dp', 'sub'), may hold values from -1 to 1
- positive_ids: int32 [16384, 16], P('dp'), may hold values from -1 to 2047, as said below
- positive_counts: int32 [16384], P('dp'), may hold values from 1 to 16
Outputs:
- losses: float32 [16384], P('dp')
- query_grad: float32 [16384, 4096], P('dp', 'sub')
- passage_grad: float32 [768, 4096], P('dp', 'sub')
- bank_grad: float32 [2048, 4096], P('dp', 'sub')
The draws below stay inside these ranges and needn't reach their ends.
Inputs may be any that keep to these rules, and one draw needn't show every extreme that they name: `positive_ids`: entries of row i before position positive_counts[i] are rows of positive_bank, the rest are -1. The valid entries of the 128 queries of one index of dp name rows held by any one index of dp at most 2 times in all (repeats counted), a bound that is reached. In each aligned block of 16 queries at most one query has more than one valid entry.
All inputs are finite; a program needn't handle non-finite values.
Results may differ from the reference program's by a relative error of at most 0.0019.
Values may be sent and summed in bfloat16 or wider, within the bound.
A program may use at most 64 MiB of HBM per device.

```python
import jax
import jax.numpy as jnp
from jax import lax

D = 4096
Q_DEV = 128
MAXPOS = 16
CAP = 2
BANK_DEV = 16
Q_TOT = 16384
P_TOT = 768
B_TOT = 2048


def joint_embed(key):
    keys = jax.random.split(jax.random.fold_in(key, 11), 2)
    spread = (2500.0 * D) ** (-0.25)
    query_draw = jax.random.normal(keys[0], (Q_TOT, D), jnp.float32) * spread
    passage_draw = jax.random.normal(keys[1], (P_TOT, D), jnp.float32) * spread
    return (jnp.clip(query_draw, -1.0, 1.0), jnp.clip(passage_draw, -1.0, 1.0))


def draw_queries(key, part):
    return joint_embed(key)[0].astype(jnp.bfloat16)


def draw_passages(key, part):
    return joint_embed(key)[1].astype(jnp.bfloat16)


def draw_positive_bank(key, part):
    keys = jax.random.split(jax.random.fold_in(key, 31), 1)
    spread = (2500.0 * D) ** (-0.25)
    bank_draw = jax.random.normal(keys[0], (B_TOT, D), jnp.float32) * spread
    return jnp.clip(bank_draw, -1.0, 1.0).astype(jnp.bfloat16)


def request_plan(key):
    keys = jax.random.split(jax.random.fold_in(key, 23), 8)
    dev_count = Q_TOT // Q_DEV
    unit_count = dev_count * CAP
    block_count = Q_DEV // 16
    is_heavy = jax.random.randint(keys[0], (dev_count, 1), 0, 2)
    big_slot = jax.random.randint(keys[1], (dev_count, block_count), 0, 16)
    heavy_count = jax.random.randint(keys[2], (dev_count, block_count), 1, MAXPOS + 1)
    light_count = jax.random.randint(keys[3], (dev_count, block_count), 1, 5)
    big_count = jnp.where(is_heavy == 1, heavy_count, light_count)
    forced_dev = jax.random.randint(keys[4], (), 0, dev_count)
    forced_block = jax.random.randint(keys[5], (), 0, block_count)
    big_count = big_count.at[forced_dev, forced_block].set(MAXPOS)
    counts = jnp.where(jnp.arange(16)[None, None, :] == big_slot[:, :, None], big_count[:, :, None], 1)
    counts = counts.reshape(dev_count, Q_DEV).astype(jnp.int32)
    hot_owner = jax.random.randint(keys[6], (), 0, dev_count)

    def per_device(dev_key, dev_counts):
        sub_keys = jax.random.split(dev_key, 3)
        is_live = (jnp.arange(MAXPOS)[None, :] < dev_counts[:, None]).reshape(-1)
        live_rank = jnp.cumsum(is_live.astype(jnp.int32)) - 1
        hot_places = jax.random.permutation(sub_keys[0], Q_DEV)[:CAP]
        is_hot = jnp.zeros((unit_count,), jnp.int32).at[hot_places].set(1)
        hot_before = jnp.cumsum(is_hot) - is_hot
        cold_order = jax.random.permutation(sub_keys[1], unit_count - CAP)
        cold_unit = cold_order[jnp.clip(jnp.arange(unit_count) - hot_before, 0, unit_count - CAP - 1)]
        cold_unit = cold_unit + CAP * (cold_unit >= hot_owner * CAP).astype(jnp.int32)
        hot_unit = hot_owner * CAP + jnp.clip(hot_before, 0, CAP - 1)
        sequence = jnp.where(is_hot == 1, hot_unit, cold_unit)
        unit_of = sequence[jnp.clip(live_rank, 0, unit_count - 1)]
        local_row = jax.random.randint(sub_keys[2], (Q_DEV * MAXPOS,), 0, BANK_DEV)
        id_rows = jnp.where(is_live, unit_of // CAP * BANK_DEV + local_row, -1)
        return id_rows.reshape(Q_DEV, MAXPOS).astype(jnp.int32)
    id_table = jax.vmap(per_device)(jax.random.split(keys[7], dev_count), counts)
    return (id_table.reshape(Q_TOT, MAXPOS), counts.reshape(Q_TOT))


def draw_positive_ids(key, part):
    return request_plan(key)[0]


def draw_positive_counts(key, part):
    return request_plan(key)[1]


def setup_inputs(seed: int = 0) -> dict:
    arg_keys = jax.random.split(jax.random.key(seed), 6)
    return {
        "queries": draw_queries(jax.random.fold_in(arg_keys[5], 71), 0),
        "passages": draw_passages(jax.random.fold_in(arg_keys[5], 71), 0),
        "positive_bank": draw_positive_bank(jax.random.fold_in(arg_keys[5], 71), 0),
        "positive_ids": draw_positive_ids(jax.random.fold_in(arg_keys[5], 71), 0),
        "positive_counts": draw_positive_counts(jax.random.fold_in(arg_keys[5], 71), 0),
    }


def reference(queries, passages, positive_bank, positive_ids, positive_counts):
    query_total, col_width = queries.shape
    bank_total = positive_bank.shape[0]
    block_rows = 1024 if query_total % 1024 == 0 else query_total
    nblocks = query_total // block_rows
    query_blocks = queries.reshape(nblocks, block_rows, col_width)
    id_blocks = positive_ids.reshape(nblocks, block_rows, MAXPOS)
    count_blocks = positive_counts.reshape(nblocks, block_rows)
    slots = jnp.arange(MAXPOS, dtype=jnp.int32)

    def accumulate(running, block_item):
        passage_sum, bank_sum = running
        block_queries, block_ids, counts = block_item
        scores = jnp.dot(block_queries, passages.T, preferred_element_type=jnp.float32) * 50.0
        is_valid = slots[None, :] < counts[:, None]
        safe_ids = jnp.clip(block_ids, 0, bank_total - 1).astype(jnp.int32)
        fetched = positive_bank[safe_ids].astype(jnp.float32)
        query_f32 = block_queries.astype(jnp.float32)
        pos_scores = jnp.einsum("kd,kpd->kp", query_f32, fetched) * 50.0
        row_max = jnp.maximum(jnp.max(scores, 1), jnp.max(jnp.where(is_valid, pos_scores, -jnp.inf), 1))
        row_total = jnp.sum(jnp.exp(scores - row_max[:, None]), 1)
        row_total = row_total + jnp.sum(jnp.exp(jnp.where(is_valid, pos_scores - row_max[:, None], -jnp.inf)), 1)
        log_total = row_max + jnp.log(row_total)
        inv_count = 1.0 / counts.astype(jnp.float32)
        query_loss = log_total - jnp.sum(jnp.where(is_valid, pos_scores, 0.0), 1) * inv_count
        weights = jnp.exp(scores - log_total[:, None]).astype(jnp.bfloat16)
        coeffs = jnp.where(is_valid, jnp.exp(jnp.where(is_valid, pos_scores - log_total[:, None], -jnp.inf)) - inv_count[:, None], 0.0)
        query_grad = 50.0 * (jnp.dot(weights, passages, preferred_element_type=jnp.float32) + jnp.einsum("kp,kpd->kd", coeffs, fetched))
        passage_sum = passage_sum + jnp.dot(weights.T, block_queries, preferred_element_type=jnp.float32)
        segment_ids = jnp.where(is_valid, safe_ids, bank_total).reshape(-1)
        contrib = (coeffs[:, :, None] * query_f32[:, None, :]).reshape(-1, col_width)
        bank_sum = bank_sum + jax.ops.segment_sum(contrib, segment_ids, bank_total + 1)[:bank_total]
        return (passage_sum, bank_sum), (query_loss, query_grad)

    start_state = (jnp.zeros((passages.shape[0], col_width), jnp.float32), jnp.zeros((bank_total, col_width), jnp.float32))
    (passage_sum, bank_sum), (loss_blocks, grad_blocks) = lax.scan(accumulate, start_state, (query_blocks, id_blocks, count_blocks))
    losses = loss_blocks.reshape(query_total)
    query_grad = grad_blocks.reshape(query_total, col_width)
    return (losses, query_grad, 50.0 * passage_sum, 50.0 * bank_sum)
```

```python
import functools

import jax
import jax.numpy as jnp
from jax import lax
from jax.experimental import pallas as pl
from jax.experimental.pallas import tpu as pltpu
from jax.sharding import PartitionSpec as P

MESH = pl.DeviceIdType.MESH
F32 = jnp.float32
BF16 = jnp.bfloat16
NZ = 16
NC = 8
SCALE = 50.0


def iota(shape, dim):
    return lax.broadcasted_iota(jnp.int32, shape, dim)


def dot(a, b, ca, cb):
    return lax.dot_general(a, b, (((ca,), (cb,)), ((), ())), preferred_element_type=F32)


def split(v):
    hi = v.astype(BF16)
    return hi, (v - hi.astype(F32)).astype(BF16)


def kernel(
    q_ref, p_ref, b_ref, ids_ref, cnt_ref,
    loss_ref, qg_ref, pg_ref, bg_ref,
    q2, bcol, pz, pb32, pz32, p32, pall,
    sel, idt, id_recv, smat, qs_send, qs_recv, pk_send, pk_recv,
    spart, sc_recv, ss_all, st_send, st_recv, pos_m, pos_e, w_all, lt_all, cf, cf_recv,
    pg_part, xg_recv, zp_part, zp_r, zp_l, bk_part, bk_r, bk_l, qx_send, qx_recv,
    q_sem, bg_s, bg_r, pg_s, pg_r, qs_s, qs_r, id_s, id_r, pk_s, pk_r, cf_s, cf_r,
    x_s, x_r, sc_s, sc_r, ss_s, ss_r, st_sem, w_s, w_r, lt_s, lt_r, xg_s, xg_r,
    br_s, br_r, pr_s, pr_r, qx_sem,
):
    dp = lax.axis_index("dp")
    j = lax.axis_index("sub")
    z = lax.div(dp, NC)
    c = lax.rem(dp, NC)
    x = lax.div(c, 2)
    yl = lax.rem(c, 2)
    yh = lax.div(j, 2)
    core = lax.rem(j, 2)
    right = lax.rem(z + 1, NZ) * NC + c
    left = lax.rem(z + NZ - 1, NZ) * NC + c
    mate = dp + 1 - 2 * yl
    plane = [z * NC + lax.rem(c + d, NC) for d in range(1, NC)]
    plane_c = [lax.rem(c + d, NC) for d in range(1, NC)]
    xs = [lax.rem(x + d, 4) for d in range(1, 4)]
    xdp = [z * NC + v * 2 + yl for v in xs]
    subs = [j + 1 - 2 * core, j + 2 - 4 * yh, 3 - j]

    def remote(src, dst, ssem, rsem, to_dp, to_sub):
        return pltpu.make_async_remote_copy(
            src_ref=src, dst_ref=dst, send_sem=ssem, recv_sem=rsem,
            device_id=(to_dp, to_sub), device_id_type=MESH,
        )

    barrier = pltpu.get_barrier_semaphore()
    for to_dp in (right, left, *plane):
        pl.semaphore_signal(barrier, inc=1, device_id=(to_dp, j), device_id_type=MESH)
    for to_sub in subs:
        pl.semaphore_signal(barrier, inc=1, device_id=(dp, to_sub), device_id_type=MESH)
    pl.semaphore_wait(barrier, 12)

    sent = []

    def go(copy):
        copy.start()
        sent.append(copy)
        return copy

    q_copy = go(remote(q_ref, q2.at[yl], q_sem.at[0], q_sem.at[1], mate, j))

    def gather_step(t, buf, own, ssem, rsem, log):
        if t > 0:
            log[t - 1][0].wait_recv()
            if t - 1 < NZ // 2 - 1:
                log[t - 1][1].wait_recv()
        if t == NZ // 2:
            return
        src = lax.rem(z + NZ - t, NZ)
        row = [go(remote(own if t == 0 else buf.at[src], buf.at[src], ssem.at[t], rsem.at[t], right, j))]
        if t < NZ // 2 - 1:
            src = lax.rem(z + t, NZ)
            k = NZ // 2 + t
            row.append(go(remote(own if t == 0 else buf.at[src], buf.at[src], ssem.at[k], rsem.at[k], left, j)))
        log.append(row)

    b_log, p_log = [], []
    p_own = p_ref[...].astype(F32)
    for k in range(8):
        pb32[k * 6 : k * 6 + 6, :] = p_own[:, k * 128 : (k + 1) * 128]
    pz[z] = pb32[...].astype(BF16)
    gather_step(0, pz, pz.at[z], pg_s, pg_r, p_log)
    gather_step(0, bcol, b_ref, bg_s, bg_r, b_log)
    bcol[z] = b_ref[...]
    q2[yl] = q_ref[...]

    def ring(t):
        gather_step(t, pz, None, pg_s, pg_r, p_log)
        gather_step(t, bcol, None, bg_s, bg_r, b_log)

    lane = iota((128, 128), 1)
    row = iota((128, 128), 0)
    eye = lane == row
    ids = ids_ref[...]
    owner = lax.shift_right_arithmetic(ids, 4)
    place = jnp.where(
        ids >= 0, (owner & 7) * 16 + lax.shift_right_arithmetic(owner, 3), -1
    )
    local = (ids & 15).astype(F32)
    many = jnp.zeros((128, 128), F32)
    w_sum = jnp.zeros((128, 128), F32)
    w_max = jnp.full((128, 128), -1.0, F32)
    for k in range(16):
        hit = place[:, k : k + 1] == lane
        w_k = local[:, k : k + 1]
        many = many + jnp.where(hit, 1.0, 0.0)
        w_sum = w_sum + jnp.where(hit, w_k, 0.0)
        w_max = jnp.maximum(w_max, jnp.where(hit, w_k, -1.0))
    ring(1)
    below = jnp.where(lane < row, 1.0, 0.0).astype(BF16)
    before = dot(below, many.astype(BF16), 1, 0)
    twice = (many > 1.5) & (before < 0.5)
    first = (many > 0.5) & (before < 0.5)
    second = ((many > 0.5) & (before > 0.5)) | twice
    w_second = jnp.where(twice, w_sum - w_max, w_max)
    id0 = jnp.sum(jnp.where(first, w_max + 1.0, 0.0), 0, keepdims=True) - 1.0
    id1 = jnp.sum(jnp.where(second, w_second + 1.0, 0.0), 0, keepdims=True) - 1.0
    sel[0] = jnp.where(first, 1.0, 0.0)
    sel[1] = jnp.where(second, 1.0, 0.0)
    tile_row = iota((8, 128), 0)
    idt[...] = jnp.where(tile_row == 0, id0, jnp.where(tile_row == 1, id1, -1.0))
    ring(2)
    id_copies = [go(remote(idt, id_recv.at[c], id_s.at[d], id_r.at[d], plane[d], j)) for d in range(7)]
    id_recv[c] = idt[...]
    for r in range(2):
        picked_q = dot(sel[r].astype(BF16), q_ref[...], 0, 0).astype(BF16)
        for k in range(NC):
            qs_send[k, r * 16 : (r + 1) * 16, :] = picked_q[k * 16 : (k + 1) * 16]
    qs_copies = [go(remote(qs_send.at[plane_c[d]], qs_recv.at[c], qs_s.at[d], qs_r.at[d], plane[d], j)) for d in range(7)]
    qs_recv[c] = qs_send[c]
    for t in range(3, NZ // 2 + 1):
        ring(t)

    pz32[...] = pz[...].reshape(NZ * 48, 128).astype(F32)
    for zz in range(NZ):
        for k in range(8):
            at = zz * 48 + k * 6
            p32[zz * 6 : zz * 6 + 6, k * 128 : (k + 1) * 128] = pz32[at : at + 6, :]
    pall[x] = p32[...].astype(BF16)
    x_copies = [go(remote(pall.at[x], pall.at[x], x_s.at[d], x_r.at[d], xdp[d], j)) for d in range(3)]

    for copy in id_copies:
        copy.wait_recv()
    lane16 = iota((16, 128), 1)
    mine = lane16 == c * 16 + iota((16, 128), 0)

    def to_column(tile_rows):
        return jnp.sum(jnp.where(mine, tile_rows, 0.0), 1, keepdims=True)

    bank_lane = iota((16, 256), 1).astype(F32) - iota((16, 256), 0).astype(F32) * 16.0
    for k in range(NC):
        for r in range(2):
            w_col = to_column(id_recv[k, r : r + 1, :])
            hot = (bank_lane == w_col) & (w_col > -0.5)
            at = k * 32 + r * 16
            smat[at : at + 16, :] = jnp.where(hot, 1.0, 0.0)
    picked_b = dot(smat[...].astype(BF16), bcol[...].reshape(256, 1024), 1, 0)
    pk_send[...] = picked_b.astype(BF16).reshape(NC, 32, 1024)
    pk_copies = [go(remote(pk_send.at[plane_c[d]], pk_recv.at[c], pk_s.at[d], pk_r.at[d], plane[d], j)) for d in range(7)]
    pk_recv[c] = pk_send[c]

    q_copy.wait_recv()
    for copy in x_copies:
        copy.wait_recv()
    part = dot(q2[...].reshape(256, 1024), pall[...].reshape(384, 1024), 1, 1)
    spart[...] = part.reshape(4, 64, 384)
    sc_copies = [go(remote(spart.at[subs[d]], sc_recv.at[d], sc_s.at[d], sc_r.at[d], dp, subs[d])) for d in range(3)]

    for copy in pk_copies:
        copy.wait_recv()

    def slots(ref, r):
        return ref[:, r * 16 : (r + 1) * 16, :].reshape(128, 1024)

    def col_to_row(v):
        return jnp.sum(jnp.where(eye, v, 0.0), 0, keepdims=True)

    def row_to_col(v):
        return jnp.sum(jnp.where(eye, v, 0.0), 1, keepdims=True)

    rows = []
    for r in range(2):
        prod = slots(qs_send, r).astype(F32) * slots(pk_recv, r).astype(F32)
        rows.append(col_to_row(jnp.sum(prod, 1, keepdims=True)))
    ss_all[j] = jnp.where(tile_row == 0, rows[0], jnp.where(tile_row == 1, rows[1], 0.0))
    ss_copies = [go(remote(ss_all.at[j], ss_all.at[j], ss_s.at[d], ss_r.at[d], dp, subs[d])) for d in range(3)]
    inv_col = 1.0 / row_to_col(cnt_ref[...].astype(F32))
    for copy in ss_copies:
        copy.wait_recv()
    ss = (((ss_all[0] + ss_all[1]) + ss_all[2]) + ss_all[3]) * SCALE
    has = [sel[r] > 0.5 for r in range(2)]
    low = [jnp.where(has[r], ss[r : r + 1], -jnp.inf) for r in range(2)]
    p_max = jnp.max(jnp.maximum(low[0], low[1]), 1, keepdims=True)
    p_exp = jnp.sum(jnp.exp(low[0] - p_max) + jnp.exp(low[1] - p_max), 1, keepdims=True)
    p_sum = jnp.sum(
        jnp.where(has[0], ss[0:1], 0.0) + jnp.where(has[1], ss[1:2], 0.0), 1, keepdims=True
    )
    pos_m[...] = jnp.broadcast_to(p_max, (128, 128))
    pos_e[...] = jnp.broadcast_to(p_exp, (128, 128))

    for copy in sc_copies:
        copy.wait_recv()
    scores = (spart[j] + sc_recv[0] + sc_recv[1] + sc_recv[2]) * SCALE
    start = pl.multiple_of(core * 64, 64)
    m_col = jnp.max(scores, 1, keepdims=True)
    here = yl == yh
    pm = jnp.where(here, pos_m[pl.ds(start, 64), 0:1], m_col)
    pe = jnp.where(here, pos_e[pl.ds(start, 64), 0:1], 0.0)
    m_all = jnp.maximum(m_col, pm)
    s_all = jnp.sum(jnp.exp(scores - m_all), 1, keepdims=True) + pe * jnp.exp(pm - m_all)
    eye64 = iota((64, 128), 1) == iota((64, 128), 0)
    m_row = jnp.sum(jnp.where(eye64, m_all, 0.0), 0, keepdims=True)
    s_row = jnp.sum(jnp.where(eye64, s_all, 0.0), 0, keepdims=True)
    st_send[...] = jnp.where(tile_row == 0, m_row, s_row)
    st_copy = go(remote(st_send, st_recv, st_sem.at[0], st_sem.at[1], mate, j))
    st_copy.wait_recv()
    m_two = jnp.sum(jnp.where(eye64, st_recv[0:1, :], 0.0), 1, keepdims=True)
    s_two = jnp.sum(jnp.where(eye64, st_recv[1:2, :], 0.0), 1, keepdims=True)
    m_top = jnp.maximum(m_all, m_two)
    total = s_all * jnp.exp(m_all - m_top) + s_two * jnp.exp(m_two - m_top)
    log_total = m_top + jnp.log(total)
    w_all[j] = jnp.exp(scores - log_total).astype(BF16)
    placed = iota((64, 128), 1) == iota((64, 128), 0) + core * 64
    lt_row = jnp.sum(jnp.where(placed, log_total, 0.0), 0, keepdims=True)
    lt_all[j] = jnp.broadcast_to(lt_row, (8, 128))
    lt_copies = [go(remote(lt_all.at[j], lt_all.at[j], lt_s.at[d], lt_r.at[d], dp, subs[d])) for d in range(3)]
    w_copies = [go(remote(w_all.at[j], w_all.at[j], w_s.at[d], w_r.at[d], dp, subs[d])) for d in range(3)]

    for copy in lt_copies:
        copy.wait_recv()
    lt_col = row_to_col(lt_all[yl * 2, 0:1, :] + lt_all[yl * 2 + 1, 0:1, :])
    coef = []
    for r in range(2):
        lt_slot = jnp.sum(jnp.where(has[r], lt_col, 0.0), 0, keepdims=True)
        inv_slot = jnp.sum(jnp.where(has[r], inv_col, 0.0), 0, keepdims=True)
        live = jnp.sum(sel[r], 0, keepdims=True) > 0.5
        coef.append(jnp.where(live, jnp.exp(jnp.where(live, ss[r : r + 1] - lt_slot, 0.0)) - inv_slot, 0.0))
    cf[...] = jnp.where(tile_row == 0, coef[0], jnp.where(tile_row == 1, coef[1], 0.0))
    cf_copies = [go(remote(cf, cf_recv.at[c], cf_s.at[d], cf_r.at[d], plane[d], j)) for d in range(7)]
    cf_recv[c] = cf[...]
    loss_ref[...] = col_to_row(lt_col - p_sum * inv_col)

    for copy in w_copies:
        copy.wait_recv()
    weights = w_all[...].reshape(256, 384)
    pg_part[...] = dot(weights, q2[...].reshape(256, 1024), 0, 0).reshape(4, 96, 1024)
    xg_copies = [go(remote(pg_part.at[xs[d]], xg_recv.at[d], xg_s.at[d], xg_r.at[d], xdp[d], j)) for d in range(3)]

    p_half = pall[...].reshape(384, 1024)
    theirs = jnp.concatenate([w_all[2 - yl * 2], w_all[3 - yl * 2]], 0)
    qx_send[...] = dot(theirs, p_half, 1, 0)
    qx_copy = go(remote(qx_send, qx_recv, qx_sem.at[0], qx_sem.at[1], mate, j))

    def scatter_step(t, part_ref, buf_r, buf_l, ssem, rsem, log):
        half = NZ // 2
        if t > 0:
            log[t - 1][0].wait_recv()
            if t - 1 < half - 1:
                log[t - 1][1].wait_recv()
        if t == half:
            return
        to_r = lax.rem(z + half - t, NZ)
        to_l = lax.rem(z + half + 1 + t, NZ)
        if t > 0:
            buf_r[t - 1] += part_ref[to_r]
            if t < half - 1:
                buf_l[t - 1] += part_ref[to_l]
        src = part_ref.at[to_r] if t == 0 else buf_r.at[t - 1]
        got = [go(remote(src, buf_r.at[t], ssem.at[t], rsem.at[t], right, j))]
        if t < half - 1:
            src = part_ref.at[to_l] if t == 0 else buf_l.at[t - 1]
            got.append(go(remote(src, buf_l.at[t], ssem.at[half + t], rsem.at[half + t], left, j)))
        log.append(got)

    br_log, pr_log = [], []
    for copy in cf_copies:
        copy.wait_recv()
    cols = []
    for k in range(NC):
        for r in range(2):
            cols.append(to_column(cf_recv[k, r : r + 1, :]))
    hi, lo = split(smat[...] * jnp.concatenate(cols, 0))
    for copy in qs_copies:
        copy.wait_recv()
    asked = qs_recv[...].reshape(256, 1024)
    bk_part[...] = (dot(hi, asked, 0, 0) + dot(lo, asked, 0, 0)).reshape(NZ, 16, 1024)
    scatter_step(0, bk_part, bk_r, bk_l, br_s, br_r, br_log)

    own = jnp.concatenate([w_all[yl * 2], w_all[yl * 2 + 1]], 0)
    mine_g = dot(own, p_half, 1, 0)
    for r in range(2):
        hi, lo = split(sel[r] * coef[r])
        rows_b = slots(pk_recv, r)
        mine_g = mine_g + dot(hi, rows_b, 1, 0) + dot(lo, rows_b, 1, 0)
    qg_ref[...] = mine_g
    scatter_step(1, bk_part, bk_r, bk_l, br_s, br_r, br_log)
    scatter_step(2, bk_part, bk_r, bk_l, br_s, br_r, br_log)
    scatter_step(3, bk_part, bk_r, bk_l, br_s, br_r, br_log)

    for copy in xg_copies:
        copy.wait_recv()
    p32[...] = pg_part[x] + xg_recv[0] + xg_recv[1] + xg_recv[2]
    zp_part[...] = jnp.zeros((NZ, 8, 1024), F32)
    for zz in range(NZ):
        zp_part[zz, 0:6, :] = p32[zz * 6 : zz * 6 + 6, :]
    scatter_step(0, zp_part, zp_r, zp_l, pr_s, pr_r, pr_log)
    for t in range(1, NZ // 2 + 1):
        if t + 3 <= NZ // 2:
            scatter_step(t + 3, bk_part, bk_r, bk_l, br_s, br_r, br_log)
        scatter_step(t, zp_part, zp_r, zp_l, pr_s, pr_r, pr_log)
    last = NZ // 2 - 1
    bg_ref[...] = SCALE * (bk_part[z] + bk_r[last] + bk_l[last - 1])
    pg_ref[...] = SCALE * (zp_part[z] + zp_r[last] + zp_l[last - 1])[0:6]
    qx_copy.wait_recv()
    qg_ref[...] = SCALE * (qg_ref[...] + qx_recv[...])
    for copy in sent:
        copy.wait_send()


def body(queries, passages, positive_bank, positive_ids, positive_counts):
    vmem = pl.BlockSpec(memory_space=pltpu.VMEM)
    dma = pltpu.SemaphoreType.DMA
    half = NZ - 1

    def buf(*shape):
        return pltpu.VMEM(shape, F32)

    def buf16(*shape):
        return pltpu.VMEM(shape, BF16)

    scratch = [
        buf16(2, 128, 1024), buf16(NZ, 16, 1024), buf16(NZ, 48, 128), buf(48, 128), buf(NZ * 48, 128),
        buf(96, 1024), buf16(4, 96, 1024),
        buf(2, 128, 128), buf(8, 128), buf(NC, 8, 128), buf(256, 256), buf16(NC, 32, 1024),
        buf16(NC, 32, 1024), buf16(NC, 32, 1024), buf16(NC, 32, 1024),
        buf(4, 64, 384), buf(3, 64, 384), buf(4, 8, 128), buf(8, 128), buf(8, 128), buf(128, 128), buf(128, 128),
        buf16(4, 64, 384), buf(4, 8, 128), buf(8, 128), buf(NC, 8, 128),
        buf(4, 96, 1024), buf(3, 96, 1024), buf(NZ, 8, 1024), buf(8, 8, 1024), buf(7, 8, 1024),
        buf(NZ, 16, 1024), buf(8, 16, 1024), buf(7, 16, 1024), buf(128, 1024), buf(128, 1024),
        dma((2,)), dma((half,)), dma((half,)), dma((half,)), dma((half,)),
        dma((7,)), dma((7,)), dma((7,)), dma((7,)), dma((7,)), dma((7,)), dma((7,)), dma((7,)),
        dma((3,)), dma((3,)), dma((3,)), dma((3,)), dma((3,)), dma((3,)), dma((2,)),
        dma((3,)), dma((3,)), dma((3,)), dma((3,)), dma((3,)), dma((3,)),
        dma((half,)), dma((half,)), dma((half,)), dma((half,)), dma((2,)),
    ]
    losses, query_grad, passage_grad, bank_grad = pl.pallas_call(
        kernel,
        out_shape=(
            jax.ShapeDtypeStruct((1, 128), F32),
            jax.ShapeDtypeStruct((128, 1024), F32),
            jax.ShapeDtypeStruct((6, 1024), F32),
            jax.ShapeDtypeStruct((16, 1024), F32),
        ),
        in_specs=[vmem] * 5,
        out_specs=(vmem,) * 4,
        scratch_shapes=scratch,
        compiler_params=pltpu.CompilerParams(
            collective_id=0, has_side_effects=True, vmem_limit_bytes=48 * 2**20
        ),
    )(queries, passages, positive_bank, positive_ids, positive_counts.reshape(1, -1))
    return losses.reshape(-1), query_grad, passage_grad, bank_grad


def solution(mesh):
    placed = (P("dp", "sub"), P("dp", "sub"), P("dp", "sub"), P("dp", None), P("dp"))
    return jax.shard_map(
        body,
        mesh=mesh,
        in_specs=placed,
        out_specs=(P("dp"), P("dp", "sub"), P("dp", "sub"), P("dp", "sub")),
        check_vma=False,
    )
```

```python
import jax
import jax.numpy as jnp
from jax import lax
from jax.experimental import pallas as pl
from jax.experimental.pallas import tpu as pltpu
from jax.sharding import PartitionSpec as P

MESH = pl.DeviceIdType.MESH
F32 = jnp.float32
BF16 = jnp.bfloat16
NZ = 16
NC = 8
SCALE = 50.0


def iota(shape, dim):
    return lax.broadcasted_iota(jnp.int32, shape, dim)


def dot(a, b, ca, cb):
    return lax.dot_general(a, b, (((ca,), (cb,)), ((), ())), preferred_element_type=F32)


def split(v):
    hi = v.astype(BF16)
    return hi, (v - hi.astype(F32)).astype(BF16)


def kernel(
    q_ref, p_ref, b_ref, ids_ref, cnt_ref,
    loss_ref, qg_ref, pg_ref, bg_ref,
    q4, bcol, pz, pb32, pz32, p32, pall,
    selt, idt, id_recv, smat, qs_send, qs_recv, pk_send, pk_recv,
    spart, sc1, sc2_send, sc2_recv, ss_all, st_all, w_all, lt_all, cf, cf_recv,
    yg_send, yg_recv, zp_part, zp_leaf, zp_chain, bk_part, bk_leaf, bk_chain, qx_send, qx_recv,
    q_s, q_r, pm_sem, bg_s, bg_r, pg_s, pg_r, qs_s, qs_r, id_s, id_r, pk_s, pk_r, cf_s, cf_r,
    sc_s, sc_r, ss_s, ss_r, st_s, st_r, w_s, w_r, lt_s, lt_r, yg_sem,
    br_s, br_r, pr_s, pr_r, qx_s, qx_r,
):
    dp = lax.axis_index("dp")
    j = lax.axis_index("sub")
    z = lax.div(dp, NC)
    c = lax.rem(dp, NC)
    x = lax.div(c, 2)
    yl = lax.rem(c, 2)
    yh = lax.div(j, 2)
    core = lax.rem(j, 2)

    def along(d):
        return lax.rem(z + NZ + d, NZ) * NC + c

    mate = dp + 1 - 2 * yl
    plane_c = [lax.rem(c + d, NC) for d in range(1, NC)]
    plane = [z * NC + v for v in plane_c]
    xs = [lax.rem(x + d, 4) for d in range(1, 4)]
    xdp = [z * NC + v * 2 + yl for v in xs]
    subs = [j + 1 - 2 * core, j + 2 - 4 * yh, 3 - j]

    barrier = pltpu.get_barrier_semaphore()
    for to_dp in (along(1), along(-1), along(2), along(-2), *plane):
        pl.semaphore_signal(barrier, inc=1, device_id=(to_dp, j), device_id_type=MESH)
    for to_sub in subs:
        pl.semaphore_signal(barrier, inc=1, device_id=(dp, to_sub), device_id_type=MESH)

    sent = []

    def go(src, dst, ssem, rsem, to_dp, to_sub):
        copy = pltpu.make_async_remote_copy(
            src_ref=src, dst_ref=dst, send_sem=ssem, recv_sem=rsem,
            device_id=(to_dp, to_sub), device_id_type=MESH,
        )
        copy.start()
        sent.append(copy)
        return copy

    p_own = p_ref[...].astype(F32)
    for k in range(8):
        pb32[k * 6 : k * 6 + 6, :] = p_own[:, k * 128 : (k + 1) * 128]
    pz[0, yl] = pb32[...].astype(BF16)
    bcol[0] = b_ref[...]
    q4[x] = q_ref[...]

    row = iota((128, 128), 0)
    lane = iota((128, 128), 1)
    eye = lane == row

    def col_to_row(v):
        return jnp.sum(jnp.where(eye, v, 0.0), 0, keepdims=True)

    def row_to_col(v):
        return jnp.sum(jnp.where(eye, v, 0.0), 1, keepdims=True)

    ids = ids_ref[...]
    owner = lax.shift_right_arithmetic(ids, 4)
    place = jnp.where(
        ids >= 0, (owner & 7) * 16 + lax.shift_right_arithmetic(owner, 3), -1
    )
    local = (ids & 15).astype(F32)
    many = jnp.zeros((128, 128), F32)
    w_sum = jnp.zeros((128, 128), F32)
    w_max = jnp.full((128, 128), -1.0, F32)
    for k in range(16):
        hit = place[k : k + 1, :] == row
        w_k = local[k : k + 1, :]
        many = many + jnp.where(hit, 1.0, 0.0)
        w_sum = w_sum + jnp.where(hit, w_k, 0.0)
        w_max = jnp.maximum(w_max, jnp.where(hit, w_k, -1.0))
    earlier = jnp.where(row < lane, 1.0, 0.0).astype(BF16)
    before = dot(many.astype(BF16), earlier, 1, 0)
    twice = (many > 1.5) & (before < 0.5)
    first = (many > 0.5) & (before < 0.5)
    second = ((many > 0.5) & (before > 0.5)) | twice
    w_second = jnp.where(twice, w_sum - w_max, w_max)
    id0 = jnp.sum(jnp.where(first, w_max + 1.0, 0.0), 1, keepdims=True) - 1.0
    id1 = jnp.sum(jnp.where(second, w_second + 1.0, 0.0), 1, keepdims=True) - 1.0
    selt[0] = jnp.where(first, 1.0, 0.0)
    selt[1] = jnp.where(second, 1.0, 0.0)
    tile_row = iota((8, 128), 0)
    idt[...] = jnp.where(tile_row == 0, col_to_row(id0), col_to_row(id1))
    id_recv[c] = idt[...]
    for r in range(2):
        picked_q = dot(selt[r].astype(BF16), q_ref[...], 1, 0).astype(BF16)
        for k in range(NC):
            qs_send[k, r * 16 : (r + 1) * 16, :] = picked_q[k * 16 : (k + 1) * 16]
    qs_recv[c] = qs_send[c]

    pl.semaphore_wait(barrier, 14)

    def gather_stage(s, buf, ssem, rsem, log):
        if s > 0:
            for copy in log[s - 1]:
                copy.wait_recv()
        if s == 4:
            return
        up = (NZ - 2 * s) % NZ
        got = [
            go(buf.at[up], buf.at[14 - 2 * s], ssem.at[4 * s], rsem.at[4 * s], along(2), j),
            go(buf.at[up], buf.at[15 - 2 * s], ssem.at[4 * s + 1], rsem.at[4 * s + 1], along(1), j),
            go(buf.at[2 * s], buf.at[2 * s + 1], ssem.at[4 * s + 2], rsem.at[4 * s + 2], along(-1), j),
        ]
        if s < 3:
            got.append(go(buf.at[2 * s], buf.at[2 * s + 2], ssem.at[4 * s + 3], rsem.at[4 * s + 3], along(-2), j))
        log.append(got)

    p_log, b_log = [], []
    pm_copy = go(pz.at[0, yl], pz.at[0, yl], pm_sem.at[0], pm_sem.at[1], mate, j)
    gather_stage(0, bcol, bg_s, bg_r, b_log)
    id_copies = [go(idt, id_recv.at[c], id_s.at[d], id_r.at[d], plane[d], j) for d in range(7)]
    q_copies = [go(q_ref, q4.at[x], q_s.at[d], q_r.at[d], xdp[d], j) for d in range(3)]
    pm_copy.wait_recv()
    gather_stage(0, pz, pg_s, pg_r, p_log)

    def spread(k):
        pz32[...] = pz[k].reshape(96, 128).astype(F32)
        for y in range(2):
            for b in range(8):
                at = y * 48 + b * 6
                to = y * 96 + k * 6
                p32[to : to + 6, b * 128 : (b + 1) * 128] = pz32[at : at + 6, :]

    spread(0)
    gather_stage(1, bcol, bg_s, bg_r, b_log)
    gather_stage(1, pz, pg_s, pg_r, p_log)
    for k in (15, 14, 1, 2):
        spread(k)
    qs_copies = [go(qs_send.at[plane_c[d]], qs_recv.at[c], qs_s.at[d], qs_r.at[d], plane[d], j) for d in range(7)]
    gather_stage(2, bcol, bg_s, bg_r, b_log)
    gather_stage(2, pz, pg_s, pg_r, p_log)
    for k in (13, 12, 3, 4):
        spread(k)

    for copy in id_copies:
        copy.wait_recv()
    mine = iota((16, 128), 1) == c * 16 + iota((16, 128), 0)

    def to_column(tile_rows):
        return jnp.sum(jnp.where(mine, tile_rows, 0.0), 1, keepdims=True)

    offset = iota((16, 256), 0) - z
    offset = jnp.where(offset < 0, offset + NZ, offset)
    bank_lane = (iota((16, 256), 1) - offset * 16).astype(F32)
    for k in range(NC):
        for r in range(2):
            w_col = to_column(id_recv[k, r : r + 1, :])
            hot = (bank_lane == w_col) & (w_col > -0.5)
            at = k * 32 + r * 16
            smat[at : at + 16, :] = jnp.where(hot, 1.0, 0.0)

    gather_stage(3, bcol, bg_s, bg_r, b_log)
    gather_stage(3, pz, pg_s, pg_r, p_log)
    for k in (11, 10, 5, 6):
        spread(k)
    gather_stage(4, bcol, bg_s, bg_r, b_log)
    picked_b = dot(smat[...].astype(BF16), bcol[...].reshape(256, 1024), 1, 0)
    pk_send[...] = picked_b.astype(BF16).reshape(NC, 32, 1024)
    pk_copies = [go(pk_send.at[plane_c[d]], pk_recv.at[c], pk_s.at[d], pk_r.at[d], plane[d], j) for d in range(7)]
    pk_recv[c] = pk_send[c]
    gather_stage(4, pz, pg_s, pg_r, p_log)
    for k in (9, 8, 7):
        spread(k)
    pall[...] = p32[...].astype(BF16)

    for copy in q_copies:
        copy.wait_recv()
    for b in range(4):
        spart[b] = dot(pall[...], q4[b], 1, 1)
    sc_copies = [go(spart.at[1 - core + 2 * h], sc1.at[h], sc_s.at[h], sc_r.at[h], dp, subs[0]) for h in range(2)]
    for copy in sc_copies:
        copy.wait_recv()
    sc2_send[...] = spart[core + 2 - 2 * yh] + sc1[1 - yh]
    sc2_copy = go(sc2_send, sc2_recv, sc_s.at[2], sc_r.at[2], dp, subs[1])

    for copy in pk_copies:
        copy.wait_recv()

    def slots(ref, r):
        return ref[:, r * 16 : (r + 1) * 16, :].reshape(128, 1024)

    rows = []
    for r in range(2):
        prod = slots(qs_send, r).astype(F32) * slots(pk_recv, r).astype(F32)
        rows.append(col_to_row(jnp.sum(prod, 1, keepdims=True)))
    ss_all[j] = jnp.where(tile_row == 0, rows[0], rows[1])
    ss_copies = [go(ss_all.at[j], ss_all.at[j], ss_s.at[d], ss_r.at[d], dp, subs[d]) for d in range(3)]
    inv_row = 1.0 / cnt_ref[...].astype(F32)
    has = [selt[r] > 0.5 for r in range(2)]
    live = [jnp.sum(selt[r], 1, keepdims=True) > 0.5 for r in range(2)]
    inv_slot = [jnp.sum(jnp.where(has[r], inv_row, 0.0), 1, keepdims=True) for r in range(2)]
    for copy in ss_copies:
        copy.wait_recv()
    ss_rows = (((ss_all[0] + ss_all[1]) + ss_all[2]) + ss_all[3]) * SCALE
    ss = [row_to_col(ss_rows[r : r + 1]) for r in range(2)]
    low = [jnp.where(has[r], ss[r], -jnp.inf) for r in range(2)]
    p_max = jnp.max(jnp.maximum(low[0], low[1]), 0, keepdims=True)
    p_exp = jnp.sum(jnp.exp(low[0] - p_max) + jnp.exp(low[1] - p_max), 0, keepdims=True)
    p_sum = jnp.sum(
        jnp.where(has[0], ss[0], 0.0) + jnp.where(has[1], ss[1], 0.0), 0, keepdims=True
    )

    sc2_copy.wait_recv()
    scores = (spart[j] + sc1[yh] + sc2_recv[...]) * SCALE
    m_own = jnp.max(scores, 0, keepdims=True)
    here = x == j
    p_top = jnp.where(here, p_max, m_own)
    p_tot = jnp.where(here, p_exp, 0.0)
    m_all = jnp.maximum(m_own, p_top)
    s_all = jnp.sum(jnp.exp(scores - m_all), 0, keepdims=True)
    s_all = s_all + p_tot * jnp.exp(p_top - m_all)
    st_all[x] = jnp.where(tile_row == 0, m_all, s_all)
    st_copies = [go(st_all.at[x], st_all.at[x], st_s.at[d], st_r.at[d], xdp[d], j) for d in range(3)]
    for copy in st_copies:
        copy.wait_recv()
    tops = [st_all[b, 0:1, :] for b in range(4)]
    m_top = jnp.maximum(jnp.maximum(tops[0], tops[1]), jnp.maximum(tops[2], tops[3]))
    total = st_all[0, 1:2, :] * jnp.exp(tops[0] - m_top)
    for b in range(1, 4):
        total = total + st_all[b, 1:2, :] * jnp.exp(tops[b] - m_top)
    log_total = m_top + jnp.log(total)
    lt_all[j] = jnp.broadcast_to(log_total, (8, 128))
    w_all[j] = jnp.exp(scores - log_total).astype(BF16)
    w_far = go(w_all.at[j], w_all.at[j], w_s.at[1], w_r.at[1], dp, subs[1])
    w_near = go(w_all.at[j], w_all.at[j], w_s.at[0], w_r.at[0], dp, subs[0])
    lt_copies = [go(lt_all.at[j], lt_all.at[j], lt_s.at[d], lt_r.at[d], dp, subs[d]) for d in range(3)]

    for copy in lt_copies:
        copy.wait_recv()
    lt_row = lt_all[x, 0:1, :]
    coef = []
    for r in range(2):
        lt_slot = jnp.sum(jnp.where(has[r], lt_row, 0.0), 1, keepdims=True)
        weight = jnp.exp(jnp.where(live[r], ss[r] - lt_slot, 0.0))
        coef.append(jnp.where(live[r], weight - inv_slot[r], 0.0))
    cf[...] = jnp.where(tile_row == 0, col_to_row(coef[0]), col_to_row(coef[1]))
    cf_copies = [go(cf, cf_recv.at[c], cf_s.at[d], cf_r.at[d], plane[d], j) for d in range(7)]
    cf_recv[c] = cf[...]
    loss_ref[...] = lt_row - p_sum * inv_row

    w_far.wait_recv()
    far = core + 2 - 2 * yh
    w_pass = go(w_all.at[far], w_all.at[far], w_s.at[2], w_r.at[2], dp, subs[0])
    w_near.wait_recv()
    w_pass.wait_recv()

    def passage_part(y):
        at = pl.multiple_of(y * 96, 96)
        acc = dot(w_all[0, pl.ds(at, 96), :], q4[0], 1, 0)
        for b in range(1, 4):
            acc = acc + dot(w_all[b, pl.ds(at, 96), :], q4[b], 1, 0)
        return acc

    yg_send[...] = passage_part(1 - yl)
    yg_copy = go(yg_send, yg_recv, yg_sem.at[0], yg_sem.at[1], mate, j)

    for copy in cf_copies:
        copy.wait_recv()
    cols = []
    for k in range(NC):
        for r in range(2):
            cols.append(to_column(cf_recv[k, r : r + 1, :]))
    hi, lo = split(smat[...] * jnp.concatenate(cols, 0))
    for copy in qs_copies:
        copy.wait_recv()
    asked = qs_recv[...].reshape(256, 1024)
    bk_part[...] = (dot(hi, asked, 0, 0) + dot(lo, asked, 0, 0)).reshape(NZ, 16, 1024)

    def leaf(i, side, part_ref, leaf_ref, ssem, rsem, log):
        k, n, to = (2 * i + 1, i, along(1)) if side == 0 else (15 - 2 * i, 4 + i, along(-1))
        log[n] = go(part_ref.at[k], leaf_ref.at[side, i], ssem.at[n], rsem.at[n], to, j)

    def chain(s, side, part_ref, leaf_ref, chain_ref, ssem, rsem, log):
        k = 8 - 2 * s if side == 0 else 8 + 2 * s
        n = 8 + 4 * side + s
        if s > (0 if side == 0 else 1):
            log[n - 1].wait_recv()
            part_ref[k] += chain_ref[side, s - 1]
        if s > 0:
            log[4 * side + 4 - s].wait_recv()
            part_ref[k] += leaf_ref[side, 4 - s]
        log[n] = go(part_ref.at[k], chain_ref.at[side, s], ssem.at[n], rsem.at[n], along(2 - 4 * side), j)

    b_args = (bk_part, bk_leaf)
    p_args = (zp_part, zp_leaf)
    b_end, p_end = (br_s, br_r, {}), (pr_s, pr_r, {})

    def start_sums(a, ch, e):
        leaf(3, 0, *a, *e)
        leaf(3, 1, *a, *e)
        chain(0, 0, *a, ch, *e)
        for i in (2, 1, 0):
            leaf(i, 0, *a, *e)
            leaf(i, 1, *a, *e)

    def sums_stage(s, a, ch, e):
        chain(s, 0, *a, ch, *e)
        chain(s, 1, *a, ch, *e)

    def sums_end(a, ch, e):
        log = e[2]
        for n in (0, 4, 11, 15):
            log[n].wait_recv()
        return a[0][0] + a[1][0, 0] + a[1][1, 0] + ch[0, 3] + ch[1, 3]

    start_sums(b_args, bk_chain, b_end)

    p32[0:96, :] = passage_part(yl)
    p_half = pall[...]
    qx_copies = []
    for d in range(3):
        qx_send[d] = dot(w_all[xs[d]], p_half, 0, 0).astype(BF16)
        qx_copies.append(go(qx_send.at[d], qx_recv.at[d], qx_s.at[d], qx_r.at[d], xdp[d], j))
    sums_stage(1, b_args, bk_chain, b_end)
    zp_part[...] = jnp.zeros((NZ, 8, 1024), F32)
    yg_copy.wait_recv()
    p32[0:96, :] = p32[0:96, :] + yg_recv[...]
    for k in range(NZ):
        zp_part[k, 0:6, :] = p32[k * 6 : k * 6 + 6, :]
    start_sums(p_args, zp_chain, p_end)

    mine_g = dot(w_all[x], p_half, 0, 0)
    for r in range(2):
        hi, lo = split(selt[r] * coef[r])
        rows_b = slots(pk_recv, r)
        mine_g = mine_g + dot(hi, rows_b, 0, 0) + dot(lo, rows_b, 0, 0)
    qg_ref[...] = mine_g
    sums_stage(2, b_args, bk_chain, b_end)
    sums_stage(1, p_args, zp_chain, p_end)
    sums_stage(3, b_args, bk_chain, b_end)
    sums_stage(2, p_args, zp_chain, p_end)
    for copy in qx_copies:
        copy.wait_recv()
    others = qx_recv[0].astype(F32) + qx_recv[1].astype(F32) + qx_recv[2].astype(F32)
    qg_ref[...] = SCALE * (qg_ref[...] + others)
    sums_stage(3, p_args, zp_chain, p_end)
    bg_ref[...] = SCALE * sums_end(b_args, bk_chain, b_end)
    pg_ref[...] = SCALE * sums_end(p_args, zp_chain, p_end)[0:6]
    for copy in sent:
        copy.wait_send()


def body(queries, passages, positive_bank, positive_ids, positive_counts):
    vmem = pl.BlockSpec(memory_space=pltpu.VMEM)
    dma = pltpu.SemaphoreType.DMA

    def buf(*shape):
        return pltpu.VMEM(shape, F32)

    def buf16(*shape):
        return pltpu.VMEM(shape, BF16)

    def sems(*counts):
        return [dma((n,)) for n in counts]

    scratch = [
        buf16(4, 128, 1024), buf16(NZ, 16, 1024), buf16(NZ, 2, 48, 128), buf(48, 128), buf(96, 128),
        buf(192, 1024), buf16(192, 1024),
        buf(2, 128, 128), buf(8, 128), buf(NC, 8, 128), buf(256, 256), buf16(NC, 32, 1024),
        buf16(NC, 32, 1024), buf16(NC, 32, 1024), buf16(NC, 32, 1024),
        buf(4, 192, 128), buf(2, 192, 128), buf(192, 128), buf(192, 128), buf(4, 8, 128), buf(4, 8, 128),
        buf16(4, 192, 128), buf(4, 8, 128), buf(8, 128), buf(NC, 8, 128),
        buf(96, 1024), buf(96, 1024), buf(NZ, 8, 1024), buf(2, 4, 8, 1024), buf(2, 4, 8, 1024),
        buf(NZ, 16, 1024), buf(2, 4, 16, 1024), buf(2, 4, 16, 1024), buf16(3, 128, 1024), buf16(3, 128, 1024),
        *sems(3, 3, 2, 16, 16, 16, 16, 7, 7, 7, 7, 7, 7, 7, 7),
        *sems(3, 3, 3, 3, 3, 3, 3, 3, 3, 3, 2),
        *sems(16, 16, 16, 16, 3, 3),
    ]
    losses, query_grad, passage_grad, bank_grad = pl.pallas_call(
        kernel,
        out_shape=(
            jax.ShapeDtypeStruct((1, 128), F32),
            jax.ShapeDtypeStruct((128, 1024), F32),
            jax.ShapeDtypeStruct((6, 1024), F32),
            jax.ShapeDtypeStruct((16, 1024), F32),
        ),
        in_specs=[vmem] * 5,
        out_specs=(vmem,) * 4,
        scratch_shapes=scratch,
        compiler_params=pltpu.CompilerParams(
            collective_id=0, has_side_effects=True, vmem_limit_bytes=48 * 2**20
        ),
    )(queries, passages, positive_bank, positive_ids.T, positive_counts.reshape(1, -1))
    return losses.reshape(-1), query_grad, passage_grad, bank_grad


def solution(mesh):
    placed = (P("dp", "sub"), P("dp", "sub"), P("dp", "sub"), P("dp", None), P("dp"))
    return jax.shard_map(
        body,
        mesh=mesh,
        in_specs=placed,
        out_specs=(P("dp"), P("dp", "sub"), P("dp", "sub"), P("dp", "sub")),
        check_vma=False,
    )
```

```python
import jax
import jax.numpy as jnp
from jax import lax
from jax.experimental import pallas as pl
from jax.experimental.pallas import tpu as pltpu
from jax.sharding import PartitionSpec as P

MESH = pl.DeviceIdType.MESH
F32 = jnp.float32
BF16 = jnp.bfloat16
NZ = 16
NC = 8
SCALE = 50.0
FAR_FIRST = (8, 7, 9, 6, 10, 5, 11, 4, 12, 3, 13, 2, 14, 1, 15)


def iota(shape, dim):
    return lax.broadcasted_iota(jnp.int32, shape, dim)


def dot(a, b, ca, cb):
    return lax.dot_general(a, b, (((ca,), (cb,)), ((), ())), preferred_element_type=F32)


def split(v):
    hi = v.astype(BF16)
    return hi, (v - hi.astype(F32)).astype(BF16)


def kernel(
    q_ref, p_ref, b_ref, ids_ref, cnt_ref,
    loss_ref, qg_ref, pg_ref, bg_ref,
    q4, bcol, pz, pb32, pz32, p32, pall,
    selt, idt, id_recv, smat, qs_send, qs_recv, pk_send, pk_recv,
    spart, sc1, sc2_send, sc2_recv, ss_all, st_all, w_all, lt_all, cf, cf_recv,
    yg_send, yg_recv, zp_part, zp_leaf, zp_chain, aq_send, aq_recv, vid, vcf, cz_send, cz_recv, qx_send, qx_recv,
    q_s, q_r, pm_sem, bg_s, bg_r, pg_s, pg_r, qs_s, qs_r, id_s, id_r, pk_s, pk_r, cf_s, cf_r,
    sc_s, sc_r, ss_s, ss_r, st_s, st_r, w_s, w_r, lt_s, lt_r, yg_s, yg_r,
    aq_s, aq_r, cz_s, cz_r, pr_s, pr_r, qx_s, qx_r,
):
    dp = lax.axis_index("dp")
    j = lax.axis_index("sub")
    z = lax.div(dp, NC)
    c = lax.rem(dp, NC)
    x = lax.div(c, 2)
    yl = lax.rem(c, 2)
    yh = lax.div(j, 2)
    core = lax.rem(j, 2)

    def along(d):
        return lax.rem(z + NZ + d, NZ) * NC + c

    mate = dp + 1 - 2 * yl
    plane_c = [lax.rem(c + d, NC) for d in range(1, NC)]
    plane = [z * NC + v for v in plane_c]
    xs = [lax.rem(x + d, 4) for d in range(1, 4)]
    xdp = [z * NC + v * 2 + yl for v in xs]
    subs = [j + 1 - 2 * core, j + 2 - 4 * yh, 3 - j]

    barrier = pltpu.get_barrier_semaphore()
    for to_dp in (along(1), along(-1), along(2), along(-2), *plane):
        pl.semaphore_signal(barrier, inc=1, device_id=(to_dp, j), device_id_type=MESH)
    for to_sub in subs:
        pl.semaphore_signal(barrier, inc=1, device_id=(dp, to_sub), device_id_type=MESH)

    sent = []

    def go(src, dst, ssem, rsem, to_dp, to_sub):
        copy = pltpu.make_async_remote_copy(
            src_ref=src, dst_ref=dst, send_sem=ssem, recv_sem=rsem,
            device_id=(to_dp, to_sub), device_id_type=MESH,
        )
        copy.start()
        sent.append(copy)
        return copy

    p_own = p_ref[...].astype(F32)
    for k in range(8):
        pb32[k * 6 : k * 6 + 6, :] = p_own[:, k * 128 : (k + 1) * 128]
    pz[0, yl] = pb32[...].astype(BF16)
    bcol[0] = b_ref[...]
    q4[x] = q_ref[...]

    row = iota((128, 128), 0)
    lane = iota((128, 128), 1)
    eye = lane == row

    def col_to_row(v):
        return jnp.sum(jnp.where(eye, v, 0.0), 0, keepdims=True)

    def row_to_col(v):
        return jnp.sum(jnp.where(eye, v, 0.0), 1, keepdims=True)

    ids = ids_ref[...]
    owner = lax.shift_right_arithmetic(ids, 4)
    place = jnp.where(
        ids >= 0, (owner & 7) * 16 + lax.shift_right_arithmetic(owner, 3), -1
    )
    local = (ids & 15).astype(F32)
    many = jnp.zeros((128, 128), F32)
    w_sum = jnp.zeros((128, 128), F32)
    w_max = jnp.full((128, 128), -1.0, F32)
    for k in range(16):
        hit = place[k : k + 1, :] == row
        w_k = local[k : k + 1, :]
        many = many + jnp.where(hit, 1.0, 0.0)
        w_sum = w_sum + jnp.where(hit, w_k, 0.0)
        w_max = jnp.maximum(w_max, jnp.where(hit, w_k, -1.0))
    earlier = jnp.where(row < lane, 1.0, 0.0).astype(BF16)
    before = dot(many.astype(BF16), earlier, 1, 0)
    twice = (many > 1.5) & (before < 0.5)
    first = (many > 0.5) & (before < 0.5)
    second = ((many > 0.5) & (before > 0.5)) | twice
    w_second = jnp.where(twice, w_sum - w_max, w_max)
    id0 = jnp.sum(jnp.where(first, w_max + 1.0, 0.0), 1, keepdims=True) - 1.0
    id1 = jnp.sum(jnp.where(second, w_second + 1.0, 0.0), 1, keepdims=True) - 1.0
    selt[0] = jnp.where(first, 1.0, 0.0)
    selt[1] = jnp.where(second, 1.0, 0.0)
    tile_row = iota((8, 128), 0)
    idt[...] = jnp.where(tile_row == 0, col_to_row(id0), col_to_row(id1))
    id_recv[c] = idt[...]
    for r in range(2):
        picked_q = dot(selt[r].astype(BF16), q_ref[...], 1, 0).astype(BF16)
        for k in range(NC):
            qs_send[k, r * 16 : (r + 1) * 16, :] = picked_q[k * 16 : (k + 1) * 16]
    qs_recv[c] = qs_send[c]

    pl.semaphore_wait(barrier, 14)

    def gather_stage(s, buf, ssem, rsem, log):
        if s > 0:
            for copy in log[s - 1]:
                copy.wait_recv()
        if s == 4:
            return
        up = (NZ - 2 * s) % NZ
        got = [
            go(buf.at[up], buf.at[14 - 2 * s], ssem.at[4 * s], rsem.at[4 * s], along(2), j),
            go(buf.at[up], buf.at[15 - 2 * s], ssem.at[4 * s + 1], rsem.at[4 * s + 1], along(1), j),
            go(buf.at[2 * s], buf.at[2 * s + 1], ssem.at[4 * s + 2], rsem.at[4 * s + 2], along(-1), j),
        ]
        if s < 3:
            got.append(go(buf.at[2 * s], buf.at[2 * s + 2], ssem.at[4 * s + 3], rsem.at[4 * s + 3], along(-2), j))
        log.append(got)

    p_log, b_log = [], []
    pm_copy = go(pz.at[0, yl], pz.at[0, yl], pm_sem.at[0], pm_sem.at[1], mate, j)
    gather_stage(0, bcol, bg_s, bg_r, b_log)
    id_copies = [go(idt, id_recv.at[c], id_s.at[d], id_r.at[d], plane[d], j) for d in range(7)]
    q_copies = [go(q_ref, q4.at[x], q_s.at[d], q_r.at[d], xdp[d], j) for d in range(3)]
    pm_copy.wait_recv()
    gather_stage(0, pz, pg_s, pg_r, p_log)

    def spread(k):
        pz32[...] = pz[k].reshape(96, 128).astype(F32)
        for y in range(2):
            for b in range(8):
                at = y * 48 + b * 6
                to = y * 96 + k * 6
                p32[to : to + 6, b * 128 : (b + 1) * 128] = pz32[at : at + 6, :]

    spread(0)
    gather_stage(1, pz, pg_s, pg_r, p_log)
    gather_stage(1, bcol, bg_s, bg_r, b_log)
    for k in (15, 14, 1, 2):
        spread(k)
    qs_copies = [go(qs_send.at[plane_c[d]], qs_recv.at[c], qs_s.at[d], qs_r.at[d], plane[d], j) for d in range(7)]
    gather_stage(2, pz, pg_s, pg_r, p_log)
    gather_stage(2, bcol, bg_s, bg_r, b_log)
    for k in (13, 12, 3, 4):
        spread(k)

    for copy in id_copies:
        copy.wait_recv()
    mine = iota((16, 128), 1) == c * 16 + iota((16, 128), 0)

    def to_column(tile_rows):
        return jnp.sum(jnp.where(mine, tile_rows, 0.0), 1, keepdims=True)

    offset = iota((16, 256), 0) - z
    offset = jnp.where(offset < 0, offset + NZ, offset)
    bank_lane = (iota((16, 256), 1) - offset * 16).astype(F32)
    slot_lane = iota((16, 128), 1) & 15
    ids_by = jnp.zeros((16, 128), F32)
    for k in range(NC):
        for r in range(2):
            w_col = to_column(id_recv[k, r : r + 1, :])
            hot = (bank_lane == w_col) & (w_col > -0.5)
            at = k * 32 + r * 16
            smat[at : at + 16, :] = jnp.where(hot, 1.0, 0.0).astype(BF16)
            ids_by = jnp.where(slot_lane == k * 2 + r, w_col + 1.0, ids_by)
    vid[...] = ids_by

    gather_stage(3, pz, pg_s, pg_r, p_log)
    gather_stage(3, bcol, bg_s, bg_r, b_log)
    for k in (11, 10, 5, 6):
        spread(k)
    gather_stage(4, pz, pg_s, pg_r, p_log)
    for k in (9, 8, 7):
        spread(k)
    pall[...] = p32[...].astype(BF16)

    for copy in q_copies:
        copy.wait_recv()
    sc_copies = []
    for h in range(2):
        b = 1 - core + 2 * h
        spart[b] = dot(pall[...], q4[b], 1, 1)
        sc_copies.append(go(spart.at[b], sc1.at[h], sc_s.at[h], sc_r.at[h], dp, subs[0]))
    for h in range(2):
        b = core + 2 * h
        spart[b] = dot(pall[...], q4[b], 1, 1)

    gather_stage(4, bcol, bg_s, bg_r, b_log)
    picked_b = dot(smat[...], bcol[...].reshape(256, 1024), 1, 0)
    pk_send[...] = picked_b.astype(BF16).reshape(NC, 32, 1024)
    pk_copies = [go(pk_send.at[plane_c[d]], pk_recv.at[c], pk_s.at[d], pk_r.at[d], plane[d], j) for d in range(7)]
    pk_recv[c] = pk_send[c]

    for copy in sc_copies:
        copy.wait_recv()
    sc2_send[...] = spart[core + 2 - 2 * yh] + sc1[1 - yh]
    sc2_copy = go(sc2_send, sc2_recv, sc_s.at[2], sc_r.at[2], dp, subs[1])

    for copy in qs_copies:
        copy.wait_recv()
    goal = iota((256, 256), 0)
    plane_of = z + lax.shift_right_logical(goal, 4)
    plane_of = jnp.where(plane_of >= NZ, plane_of - NZ, plane_of)
    goal = (lax.shift_right_logical(goal, 1) & 7) * 32 + (goal & 1) * 16 + plane_of
    order = jnp.where(iota((256, 256), 1) == goal, 1.0, 0.0).astype(BF16)
    by_plane = dot(order, qs_recv[...].reshape(256, 1024), 1, 0)
    aq_send[...] = by_plane.astype(BF16).reshape(NZ, 16, 1024)
    aq_recv[0] = aq_send[0]
    aq_copies = [go(aq_send.at[k], aq_recv.at[NZ - k], aq_s.at[k - 1], aq_r.at[NZ - k - 1], along(k), j) for k in FAR_FIRST]

    for copy in pk_copies:
        copy.wait_recv()

    def slots(ref, r):
        return ref[:, r * 16 : (r + 1) * 16, :].reshape(128, 1024)

    rows = []
    for r in range(2):
        prod = slots(qs_send, r).astype(F32) * slots(pk_recv, r).astype(F32)
        rows.append(col_to_row(jnp.sum(prod, 1, keepdims=True)))
    ss_all[j] = jnp.where(tile_row == 0, rows[0], rows[1])
    ss_copies = [go(ss_all.at[j], ss_all.at[j], ss_s.at[d], ss_r.at[d], dp, subs[d]) for d in range(3)]
    inv_row = 1.0 / cnt_ref[...].astype(F32)
    has = [selt[r] > 0.5 for r in range(2)]
    live = [jnp.sum(selt[r], 1, keepdims=True) > 0.5 for r in range(2)]
    inv_slot = [jnp.sum(jnp.where(has[r], inv_row, 0.0), 1, keepdims=True) for r in range(2)]
    for copy in ss_copies:
        copy.wait_recv()
    ss_rows = (((ss_all[0] + ss_all[1]) + ss_all[2]) + ss_all[3]) * SCALE
    ss = [row_to_col(ss_rows[r : r + 1]) for r in range(2)]
    low = [jnp.where(has[r], ss[r], -jnp.inf) for r in range(2)]
    p_max = jnp.max(jnp.maximum(low[0], low[1]), 0, keepdims=True)
    p_exp = jnp.sum(jnp.exp(low[0] - p_max) + jnp.exp(low[1] - p_max), 0, keepdims=True)
    p_sum = jnp.sum(
        jnp.where(has[0], ss[0], 0.0) + jnp.where(has[1], ss[1], 0.0), 0, keepdims=True
    )

    sc2_copy.wait_recv()
    scores = (spart[j] + sc1[yh] + sc2_recv[...]) * SCALE
    m_own = jnp.max(scores, 0, keepdims=True)
    here = x == j
    p_top = jnp.where(here, p_max, m_own)
    p_tot = jnp.where(here, p_exp, 0.0)
    m_all = jnp.maximum(m_own, p_top)
    s_all = jnp.sum(jnp.exp(scores - m_all), 0, keepdims=True)
    s_all = s_all + p_tot * jnp.exp(p_top - m_all)
    st_all[x] = jnp.where(tile_row == 0, m_all, s_all)
    st_copies = [go(st_all.at[x], st_all.at[x], st_s.at[d], st_r.at[d], xdp[d], j) for d in range(3)]
    for copy in st_copies:
        copy.wait_recv()
    tops = [st_all[b, 0:1, :] for b in range(4)]
    m_top = jnp.maximum(jnp.maximum(tops[0], tops[1]), jnp.maximum(tops[2], tops[3]))
    total = st_all[0, 1:2, :] * jnp.exp(tops[0] - m_top)
    for b in range(1, 4):
        total = total + st_all[b, 1:2, :] * jnp.exp(tops[b] - m_top)
    log_total = m_top + jnp.log(total)
    lt_all[j] = jnp.broadcast_to(log_total, (8, 128))
    w_all[j] = jnp.exp(scores - log_total).astype(BF16)
    w_far = go(w_all.at[j], w_all.at[j], w_s.at[1], w_r.at[1], dp, subs[1])
    w_near = go(w_all.at[j], w_all.at[j], w_s.at[0], w_r.at[0], dp, subs[0])
    lt_copies = [go(lt_all.at[j], lt_all.at[j], lt_s.at[d], lt_r.at[d], dp, subs[d]) for d in range(3)]

    for copy in lt_copies:
        copy.wait_recv()
    lt_row = lt_all[x, 0:1, :]
    coef = []
    for r in range(2):
        lt_slot = jnp.sum(jnp.where(has[r], lt_row, 0.0), 1, keepdims=True)
        weight = jnp.exp(jnp.where(live[r], ss[r] - lt_slot, 0.0))
        coef.append(jnp.where(live[r], weight - inv_slot[r], 0.0))
    cf[...] = jnp.where(tile_row == 0, col_to_row(coef[0]), col_to_row(coef[1]))
    cf_copies = [go(cf, cf_recv.at[c], cf_s.at[d], cf_r.at[d], plane[d], j) for d in range(7)]
    cf_recv[c] = cf[...]
    loss_ref[...] = lt_row - p_sum * inv_row

    w_far.wait_recv()
    far = core + 2 - 2 * yh
    w_pass = go(w_all.at[far], w_all.at[far], w_s.at[2], w_r.at[2], dp, subs[0])
    w_near.wait_recv()
    w_pass.wait_recv()

    def passage_part(y):
        at = pl.multiple_of(y * 96, 96)
        acc = dot(w_all[0, pl.ds(at, 96), :], q4[0], 1, 0)
        for b in range(1, 4):
            acc = acc + dot(w_all[b, pl.ds(at, 96), :], q4[b], 1, 0)
        return acc

    yg_send[...] = passage_part(1 - yl)
    yg_copies = []
    for n, (at, size) in enumerate(((24, 48), (0, 24), (72, 24))):
        piece = pl.ds(at, size)
        yg_copies.append(go(yg_send.at[piece], yg_recv.at[piece], yg_s.at[n], yg_r.at[n], mate, j))

    for copy in cf_copies:
        copy.wait_recv()
    cf_by = jnp.zeros((16, 128), F32)
    for k in range(NC):
        for r in range(2):
            cf_by = jnp.where(slot_lane == k * 2 + r, to_column(cf_recv[k, r : r + 1, :]), cf_by)
    vcf[...] = cf_by
    tile_group = lax.shift_right_logical(iota((8, 128), 1), 4)
    for k in range(NZ):
        oz = lax.rem(z + k, NZ)
        m = (NZ - k) % NZ
        here_cf = (tile_row == m // 8) & (tile_group == m % 8)
        here_id = (tile_row == m // 8 + 2) & (tile_group == m % 8)
        tile = jnp.where(here_cf, vcf[pl.ds(oz, 1), :], 0.0)
        cz_send[k] = jnp.where(here_id, vid[pl.ds(oz, 1), :], tile)
    cz_recv[0] = cz_send[0]
    cz_copies = [go(cz_send.at[k], cz_recv.at[NZ - k], cz_s.at[k - 1], cz_r.at[NZ - k - 1], along(k), j) for k in FAR_FIRST]

    def leaf(i, side, part_ref, leaf_ref, ssem, rsem, log):
        k, n, to = (2 * i + 1, i, along(1)) if side == 0 else (15 - 2 * i, 4 + i, along(-1))
        log[n] = go(part_ref.at[k], leaf_ref.at[side, i], ssem.at[n], rsem.at[n], to, j)

    def chain(s, side, part_ref, leaf_ref, chain_ref, ssem, rsem, log):
        k = 8 - 2 * s if side == 0 else 8 + 2 * s
        n = 8 + 4 * side + s
        if s > (0 if side == 0 else 1):
            log[n - 1].wait_recv()
            part_ref[k] += chain_ref[side, s - 1]
        if s > 0:
            log[4 * side + 4 - s].wait_recv()
            part_ref[k] += leaf_ref[side, 4 - s]
        log[n] = go(part_ref.at[k], chain_ref.at[side, s], ssem.at[n], rsem.at[n], along(2 - 4 * side), j)

    sums = (zp_part, zp_leaf)
    ends = (pr_s, pr_r, {})

    def sums_stage(s):
        chain(s, 0, *sums, zp_chain, *ends)
        if s > 0:
            chain(s, 1, *sums, zp_chain, *ends)

    def leaves(i):
        leaf(i, 0, *sums, *ends)
        leaf(i, 1, *sums, *ends)

    def both_halves(k):
        at = slice(k * 6, k * 6 + 6)
        zp_part[k, 0:6, :] = p32[at, :] + yg_recv[at, :]

    zp_part[...] = jnp.zeros((NZ, 8, 1024), F32)
    p32[0:96, :] = passage_part(yl)
    p_half = pall[...]
    qx_copies = []
    for d in range(3):
        qx_send[d] = dot(w_all[xs[d]], p_half, 0, 0).astype(BF16)
        qx_copies.append(go(qx_send.at[d], qx_recv.at[d], qx_s.at[d], qx_r.at[d], xdp[d], j))
    yg_copies[0].wait_recv()
    for k in range(4, 12):
        both_halves(k)
    leaves(3)
    sums_stage(0)
    leaves(2)

    mine_g = dot(w_all[x], p_half, 0, 0)
    for r in range(2):
        hi, lo = split(selt[r] * coef[r])
        rows_b = slots(pk_recv, r)
        mine_g = mine_g + dot(hi, rows_b, 0, 0) + dot(lo, rows_b, 0, 0)
    qg_ref[...] = mine_g
    sums_stage(1)
    for copy in yg_copies[1:]:
        copy.wait_recv()
    for k in (0, 1, 2, 3, 12, 13, 14, 15):
        both_halves(k)
    leaves(1)
    leaves(0)

    for copy in cz_copies + aq_copies:
        copy.wait_recv()
    tiles = cz_recv[0]
    for k in range(1, NZ):
        tiles = tiles + cz_recv[k]
    bank_sum = jnp.zeros((16, 1024), F32)
    bank_row = (iota((16, 128), 0) + 1).astype(F32)
    for h in range(2):
        hi, lo = split(jnp.where(tiles[h + 2 : h + 3] == bank_row, tiles[h : h + 1], 0.0))
        asked = aq_recv[8 * h : 8 * h + 8].reshape(128, 1024)
        bank_sum = bank_sum + dot(hi, asked, 1, 0) + dot(lo, asked, 1, 0)
    bg_ref[...] = SCALE * bank_sum
    sums_stage(2)
    for copy in qx_copies:
        copy.wait_recv()
    others = qx_recv[0].astype(F32) + qx_recv[1].astype(F32) + qx_recv[2].astype(F32)
    qg_ref[...] = SCALE * (qg_ref[...] + others)
    sums_stage(3)
    for n in (0, 4, 11, 15):
        ends[2][n].wait_recv()
    total_p = zp_part[0] + zp_leaf[0, 0] + zp_leaf[1, 0] + zp_chain[0, 3] + zp_chain[1, 3]
    pg_ref[...] = SCALE * total_p[0:6]
    for copy in sent:
        copy.wait_send()


def body(queries, passages, positive_bank, positive_ids, positive_counts):
    vmem = pl.BlockSpec(memory_space=pltpu.VMEM)
    dma = pltpu.SemaphoreType.DMA

    def buf(*shape):
        return pltpu.VMEM(shape, F32)

    def buf16(*shape):
        return pltpu.VMEM(shape, BF16)

    def sems(*counts):
        return [dma((n,)) for n in counts]

    scratch = [
        buf16(4, 128, 1024), buf16(NZ, 16, 1024), buf16(NZ, 2, 48, 128), buf(48, 128), buf(96, 128),
        buf(192, 1024), buf16(192, 1024),
        buf(2, 128, 128), buf(8, 128), buf(NC, 8, 128), buf16(256, 256), buf16(NC, 32, 1024),
        buf16(NC, 32, 1024), buf16(NC, 32, 1024), buf16(NC, 32, 1024),
        buf(4, 192, 128), buf(2, 192, 128), buf(192, 128), buf(192, 128), buf(4, 8, 128), buf(4, 8, 128),
        buf16(4, 192, 128), buf(4, 8, 128), buf(8, 128), buf(NC, 8, 128),
        buf(96, 1024), buf(96, 1024), buf(NZ, 8, 1024), buf(2, 4, 8, 1024), buf(2, 4, 8, 1024),
        buf16(NZ, 16, 1024), buf16(NZ, 16, 1024), buf(16, 128), buf(16, 128), buf(NZ, 8, 128), buf(NZ, 8, 128),
        buf16(3, 128, 1024), buf16(3, 128, 1024),
        *sems(3, 3, 2, 16, 16, 16, 16, 7, 7, 7, 7, 7, 7, 7, 7),
        *sems(3, 3, 3, 3, 3, 3, 3, 3, 3, 3, 3, 3),
        *sems(15, 15, 15, 15, 16, 16, 3, 3),
    ]
    losses, query_grad, passage_grad, bank_grad = pl.pallas_call(
        kernel,
        out_shape=(
            jax.ShapeDtypeStruct((1, 128), F32),
            jax.ShapeDtypeStruct((128, 1024), F32),
            jax.ShapeDtypeStruct((6, 1024), F32),
            jax.ShapeDtypeStruct((16, 1024), F32),
        ),
        in_specs=[vmem] * 5,
        out_specs=(vmem,) * 4,
        scratch_shapes=scratch,
        compiler_params=pltpu.CompilerParams(
            collective_id=0, has_side_effects=True, vmem_limit_bytes=48 * 2**20
        ),
    )(queries, passages, positive_bank, positive_ids.T, positive_counts.reshape(1, -1))
    return losses.reshape(-1), query_grad, passage_grad, bank_grad


def solution(mesh):
    placed = (P("dp", "sub"), P("dp", "sub"), P("dp", "sub"), P("dp", None), P("dp"))
    return jax.shard_map(
        body,
        mesh=mesh,
        in_specs=placed,
        out_specs=(P("dp"), P("dp", "sub"), P("dp", "sub"), P("dp", "sub")),
        check_vma=False,
    )
```

```python
import jax
import jax.numpy as jnp
from jax import lax
from jax.experimental import pallas as pl
from jax.experimental.pallas import tpu as pltpu
from jax.sharding import PartitionSpec as P

MESH = pl.DeviceIdType.MESH
F32 = jnp.float32
BF16 = jnp.bfloat16
NZ = 16
NC = 8
SCALE = 50.0
FAR_FIRST = (8, 7, 9, 6, 10, 5, 11, 4, 12, 3, 13, 2, 14, 1, 15)


def iota(shape, dim):
    return lax.broadcasted_iota(jnp.int32, shape, dim)


def dot(a, b, ca, cb):
    return lax.dot_general(a, b, (((ca,), (cb,)), ((), ())), preferred_element_type=F32)


def split(v):
    hi = v.astype(BF16)
    return hi, (v - hi.astype(F32)).astype(BF16)


def kernel(
    q_ref, p_ref, b_ref, ids_ref, cnt_ref,
    loss_ref, qg_ref, pg_ref, bg_ref,
    q4, bcol, pz, pb32, pz32, p32, pall,
    selt, idt, id_recv, smat, qs_send, qs_recv, pk_send, pk_recv,
    spart, sc1, sc2_send, sc2_recv, ss_all, st_all, w_all, lt_all, cf, cf_recv,
    yg_send, yg_recv, yg32, zp_part, zp_leaf, zp_chain, aq_send, aq_recv, vid, vcf, cz_send, cz_recv, qx_send, qx_recv,
    q_s, q_r, pm_sem, bg_s, bg_r, pg_s, pg_r, qs_s, qs_r, id_s, id_r, pk_s, pk_r, cf_s, cf_r,
    sc_s, sc_r, ss_s, ss_r, st_s, st_r, w_s, w_r, lt_s, lt_r, yg_s, yg_r,
    aq_s, aq_r, cz_s, cz_r, pr_s, pr_r, qx_s, qx_r, in_sem,
):
    dp = lax.axis_index("dp")
    j = lax.axis_index("sub")
    z = lax.div(dp, NC)
    c = lax.rem(dp, NC)
    x = lax.div(c, 2)
    yl = lax.rem(c, 2)
    yh = lax.div(j, 2)
    core = lax.rem(j, 2)

    def along(d):
        return lax.rem(z + NZ + d, NZ) * NC + c

    mate = dp + 1 - 2 * yl
    plane_c = [lax.rem(c + d, NC) for d in range(1, NC)]
    plane = [z * NC + v for v in plane_c]
    xs = [lax.rem(x + d, 4) for d in range(1, 4)]
    xdp = [z * NC + v * 2 + yl for v in xs]
    subs = [j + 1 - 2 * core, j + 2 - 4 * yh, 3 - j]

    barrier = pltpu.get_barrier_semaphore()
    for to_dp in (along(1), along(-1), along(2), along(-2), *plane):
        pl.semaphore_signal(barrier, inc=1, device_id=(to_dp, j), device_id_type=MESH)
    for to_sub in subs:
        pl.semaphore_signal(barrier, inc=1, device_id=(dp, to_sub), device_id_type=MESH)

    sent = []

    def go(src, dst, ssem, rsem, to_dp, to_sub):
        copy = pltpu.make_async_remote_copy(
            src_ref=src, dst_ref=dst, send_sem=ssem, recv_sem=rsem,
            device_id=(to_dp, to_sub), device_id_type=MESH,
        )
        copy.start()
        sent.append(copy)
        return copy

    fetch_q = pltpu.make_async_copy(q_ref, q4.at[x], in_sem.at[0])
    fetch_b = pltpu.make_async_copy(b_ref, bcol.at[0], in_sem.at[1])
    fetch_q.start()
    fetch_b.start()

    p_own = p_ref[...].astype(F32)
    for k in range(8):
        pb32[k * 6 : k * 6 + 6, :] = p_own[:, k * 128 : (k + 1) * 128]
    pz[0, yl] = pb32[...].astype(BF16)

    row = iota((128, 128), 0)
    lane = iota((128, 128), 1)
    eye = lane == row

    def col_to_row(v):
        return jnp.sum(jnp.where(eye, v, 0.0), 0, keepdims=True)

    def row_to_col(v):
        return jnp.sum(jnp.where(eye, v, 0.0), 1, keepdims=True)

    ids = ids_ref[...]
    owner = lax.shift_right_arithmetic(ids, 4)
    place = jnp.where(
        ids >= 0, (owner & 7) * 16 + lax.shift_right_arithmetic(owner, 3), -1
    )
    local = (ids & 15).astype(F32)
    many = jnp.zeros((128, 128), F32)
    w_sum = jnp.zeros((128, 128), F32)
    w_max = jnp.full((128, 128), -1.0, F32)
    for k in range(16):
        hit = place[k : k + 1, :] == row
        w_k = local[k : k + 1, :]
        many = many + jnp.where(hit, 1.0, 0.0)
        w_sum = w_sum + jnp.where(hit, w_k, 0.0)
        w_max = jnp.maximum(w_max, jnp.where(hit, w_k, -1.0))
    earlier = jnp.where(row < lane, 1.0, 0.0).astype(BF16)
    before = dot(many.astype(BF16), earlier, 1, 0)
    twice = (many > 1.5) & (before < 0.5)
    first = (many > 0.5) & (before < 0.5)
    second = ((many > 0.5) & (before > 0.5)) | twice
    w_second = jnp.where(twice, w_sum - w_max, w_max)
    id0 = jnp.sum(jnp.where(first, w_max + 1.0, 0.0), 1, keepdims=True) - 1.0
    id1 = jnp.sum(jnp.where(second, w_second + 1.0, 0.0), 1, keepdims=True) - 1.0
    selt[0] = jnp.where(first, 1.0, 0.0)
    selt[1] = jnp.where(second, 1.0, 0.0)
    tile_row = iota((8, 128), 0)
    idt[...] = jnp.where(tile_row == 0, col_to_row(id0), col_to_row(id1))
    id_recv[c] = idt[...]
    fetch_q.wait()
    fetch_b.wait()
    for r in range(2):
        picked_q = dot(selt[r].astype(BF16), q4[x], 1, 0).astype(BF16)
        for k in range(NC):
            qs_send[k, r * 16 : (r + 1) * 16, :] = picked_q[k * 16 : (k + 1) * 16]
    qs_recv[c] = qs_send[c]

    pl.semaphore_wait(barrier, 14)

    def gather_stage(s, buf, ssem, rsem, log):
        if s > 0:
            log[s - 1][0].wait_recv()
            if s < 4:
                log[s - 1][3].wait_recv()
        if s == 4:
            return
        up = (NZ - 2 * s) % NZ
        got = [
            go(buf.at[up], buf.at[14 - 2 * s], ssem.at[4 * s], rsem.at[4 * s], along(2), j),
        ]
        far = None
        if s < 3:
            far = go(buf.at[2 * s], buf.at[2 * s + 2], ssem.at[4 * s + 3], rsem.at[4 * s + 3], along(-2), j)
        got += [
            go(buf.at[up], buf.at[15 - 2 * s], ssem.at[4 * s + 1], rsem.at[4 * s + 1], along(1), j),
            go(buf.at[2 * s], buf.at[2 * s + 1], ssem.at[4 * s + 2], rsem.at[4 * s + 2], along(-1), j),
            far,
        ]
        log.append(got)

    def sides(s, log):
        log[s][1].wait_recv()
        log[s][2].wait_recv()

    p_log, b_log = [], []
    pm_copy = go(pz.at[0, yl], pz.at[0, yl], pm_sem.at[0], pm_sem.at[1], mate, j)
    gather_stage(0, bcol, bg_s, bg_r, b_log)
    id_copies = [go(idt, id_recv.at[c], id_s.at[d], id_r.at[d], plane[d], j) for d in range(7)]
    q_copies = [go(q4.at[x], q4.at[x], q_s.at[d], q_r.at[d], xdp[d], j) for d in range(3)]
    pm_copy.wait_recv()
    gather_stage(0, pz, pg_s, pg_r, p_log)

    def spread(k):
        pz32[...] = pz[k].reshape(96, 128).astype(F32)
        for y in range(2):
            for b in range(8):
                at = y * 48 + b * 6
                to = y * 96 + k * 6
                p32[to : to + 6, b * 128 : (b + 1) * 128] = pz32[at : at + 6, :]

    spread(0)
    gather_stage(1, pz, pg_s, pg_r, p_log)
    gather_stage(1, bcol, bg_s, bg_r, b_log)
    sides(0, p_log)
    for k in (15, 14, 1, 2):
        spread(k)
    qs_copies = [go(qs_send.at[plane_c[d]], qs_recv.at[c], qs_s.at[d], qs_r.at[d], plane[d], j) for d in range(7)]
    gather_stage(2, pz, pg_s, pg_r, p_log)
    gather_stage(2, bcol, bg_s, bg_r, b_log)
    sides(1, p_log)
    for k in (13, 12, 3, 4):
        spread(k)

    for copy in id_copies:
        copy.wait_recv()
    mine = iota((16, 128), 1) == c * 16 + iota((16, 128), 0)

    def to_column(tile_rows):
        return jnp.sum(jnp.where(mine, tile_rows, 0.0), 1, keepdims=True)

    offset = iota((16, 256), 0) - z
    offset = jnp.where(offset < 0, offset + NZ, offset)
    bank_lane = (iota((16, 256), 1) - offset * 16).astype(F32)
    slot_lane = iota((16, 128), 1) & 15
    ids_by = jnp.zeros((16, 128), F32)
    for k in range(NC):
        for r in range(2):
            w_col = to_column(id_recv[k, r : r + 1, :])
            hot = (bank_lane == w_col) & (w_col > -0.5)
            at = k * 32 + r * 16
            smat[at : at + 16, :] = jnp.where(hot, 1.0, 0.0).astype(BF16)
            ids_by = jnp.where(slot_lane == k * 2 + r, w_col + 1.0, ids_by)
    vid[...] = ids_by

    gather_stage(3, pz, pg_s, pg_r, p_log)
    gather_stage(3, bcol, bg_s, bg_r, b_log)
    sides(2, p_log)
    for k in (11, 10, 5, 6):
        spread(k)
    gather_stage(4, pz, pg_s, pg_r, p_log)
    sides(3, p_log)
    for k in (9, 8, 7):
        spread(k)
    pall[...] = p32[...].astype(BF16)

    for copy in q_copies:
        copy.wait_recv()
    sc_copies = []
    for h in range(2):
        b = 1 - core + 2 * h
        spart[b] = dot(pall[...], q4[b], 1, 1)
        sc_copies.append(go(spart.at[b], sc1.at[h], sc_s.at[h], sc_r.at[h], dp, subs[0]))
    for h in range(2):
        b = core + 2 * h
        spart[b] = dot(pall[...], q4[b], 1, 1)

    gather_stage(4, bcol, bg_s, bg_r, b_log)
    for n in range(4):
        sides(n, b_log)
    picked_b = dot(smat[...], bcol[...].reshape(256, 1024), 1, 0)
    pk_send[...] = picked_b.astype(BF16).reshape(NC, 32, 1024)
    pk_copies = [go(pk_send.at[plane_c[d]], pk_recv.at[c], pk_s.at[d], pk_r.at[d], plane[d], j) for d in range(7)]
    pk_recv[c] = pk_send[c]

    for copy in sc_copies:
        copy.wait_recv()
    sc2_send[...] = spart[core + 2 - 2 * yh] + sc1[1 - yh]
    sc2_copy = go(sc2_send, sc2_recv, sc_s.at[2], sc_r.at[2], dp, subs[1])

    for copy in qs_copies:
        copy.wait_recv()
    goal = iota((256, 256), 0)
    plane_of = z + lax.shift_right_logical(goal, 4)
    plane_of = jnp.where(plane_of >= NZ, plane_of - NZ, plane_of)
    goal = (lax.shift_right_logical(goal, 1) & 7) * 32 + (goal & 1) * 16 + plane_of
    order = jnp.where(iota((256, 256), 1) == goal, 1.0, 0.0).astype(BF16)
    by_plane = dot(order, qs_recv[...].reshape(256, 1024), 1, 0)
    aq_send[...] = by_plane.astype(BF16).reshape(NZ, 16, 1024)
    aq_recv[0] = aq_send[0]
    aq_copies = [go(aq_send.at[k], aq_recv.at[NZ - k], aq_s.at[k - 1], aq_r.at[NZ - k - 1], along(k), j) for k in FAR_FIRST]

    for copy in pk_copies:
        copy.wait_recv()

    def slots(ref, r):
        return ref[:, r * 16 : (r + 1) * 16, :].reshape(128, 1024)

    rows = []
    for r in range(2):
        prod = slots(qs_send, r).astype(F32) * slots(pk_recv, r).astype(F32)
        rows.append(col_to_row(jnp.sum(prod, 1, keepdims=True)))
    ss_all[j] = jnp.where(tile_row == 0, rows[0], rows[1])
    ss_copies = [go(ss_all.at[j], ss_all.at[j], ss_s.at[d], ss_r.at[d], dp, subs[d]) for d in range(3)]
    inv_row = 1.0 / cnt_ref[...].astype(F32)
    has = [selt[r] > 0.5 for r in range(2)]
    live = [jnp.sum(selt[r], 1, keepdims=True) > 0.5 for r in range(2)]
    inv_slot = [jnp.sum(jnp.where(has[r], inv_row, 0.0), 1, keepdims=True) for r in range(2)]
    for copy in ss_copies:
        copy.wait_recv()
    ss_rows = (((ss_all[0] + ss_all[1]) + ss_all[2]) + ss_all[3]) * SCALE
    ss = [row_to_col(ss_rows[r : r + 1]) for r in range(2)]
    low = [jnp.where(has[r], ss[r], -jnp.inf) for r in range(2)]
    p_max = jnp.max(jnp.maximum(low[0], low[1]), 0, keepdims=True)
    p_exp = jnp.sum(jnp.exp(low[0] - p_max) + jnp.exp(low[1] - p_max), 0, keepdims=True)
    p_sum = jnp.sum(
        jnp.where(has[0], ss[0], 0.0) + jnp.where(has[1], ss[1], 0.0), 0, keepdims=True
    )

    sc2_copy.wait_recv()
    scores = (spart[j] + sc1[yh] + sc2_recv[...]) * SCALE
    m_own = jnp.max(scores, 0, keepdims=True)
    here = x == j
    p_top = jnp.where(here, p_max, m_own)
    p_tot = jnp.where(here, p_exp, 0.0)
    m_all = jnp.maximum(m_own, p_top)
    s_all = jnp.sum(jnp.exp(scores - m_all), 0, keepdims=True)
    s_all = s_all + p_tot * jnp.exp(p_top - m_all)
    st_all[x] = jnp.where(tile_row == 0, m_all, s_all)
    st_copies = [go(st_all.at[x], st_all.at[x], st_s.at[d], st_r.at[d], xdp[d], j) for d in range(3)]
    for copy in st_copies:
        copy.wait_recv()
    tops = [st_all[b, 0:1, :] for b in range(4)]
    m_top = jnp.maximum(jnp.maximum(tops[0], tops[1]), jnp.maximum(tops[2], tops[3]))
    total = st_all[0, 1:2, :] * jnp.exp(tops[0] - m_top)
    for b in range(1, 4):
        total = total + st_all[b, 1:2, :] * jnp.exp(tops[b] - m_top)
    log_total = m_top + jnp.log(total)
    lt_all[j] = jnp.broadcast_to(log_total, (8, 128))
    w_all[j] = jnp.exp(scores - log_total).astype(BF16)
    w_far = go(w_all.at[j], w_all.at[j], w_s.at[1], w_r.at[1], dp, subs[1])
    w_near = go(w_all.at[j], w_all.at[j], w_s.at[0], w_r.at[0], dp, subs[0])
    lt_copies = [go(lt_all.at[j], lt_all.at[j], lt_s.at[d], lt_r.at[d], dp, subs[d]) for d in range(3)]

    w_far.wait_recv()
    far = core + 2 - 2 * yh
    w_pass = go(w_all.at[far], w_all.at[far], w_s.at[2], w_r.at[2], dp, subs[0])
    for copy in lt_copies:
        copy.wait_recv()
    lt_row = lt_all[x, 0:1, :]
    coef = []
    for r in range(2):
        lt_slot = jnp.sum(jnp.where(has[r], lt_row, 0.0), 1, keepdims=True)
        weight = jnp.exp(jnp.where(live[r], ss[r] - lt_slot, 0.0))
        coef.append(jnp.where(live[r], weight - inv_slot[r], 0.0))
    cf[...] = jnp.where(tile_row == 0, col_to_row(coef[0]), col_to_row(coef[1]))
    cf_copies = [go(cf, cf_recv.at[c], cf_s.at[d], cf_r.at[d], plane[d], j) for d in range(7)]
    cf_recv[c] = cf[...]
    loss_ref[...] = lt_row - p_sum * inv_row

    w_near.wait_recv()
    w_pass.wait_recv()

    def passage_part(y):
        at = pl.multiple_of(y * 96, 96)
        acc = dot(w_all[0, pl.ds(at, 96), :], q4[0], 1, 0)
        for b in range(1, 4):
            acc = acc + dot(w_all[b, pl.ds(at, 96), :], q4[b], 1, 0)
        return acc

    yg_send[...] = passage_part(1 - yl).astype(BF16)
    yg_copies = []
    for n, (at, size) in enumerate(((16, 64), (0, 16), (80, 16))):
        piece = pl.ds(at, size)
        yg_copies.append(go(yg_send.at[piece], yg_recv.at[piece], yg_s.at[n], yg_r.at[n], mate, j))

    for copy in cf_copies:
        copy.wait_recv()
    cf_by = jnp.zeros((16, 128), F32)
    for k in range(NC):
        for r in range(2):
            cf_by = jnp.where(slot_lane == k * 2 + r, to_column(cf_recv[k, r : r + 1, :]), cf_by)
    vcf[...] = cf_by
    tile_group = lax.shift_right_logical(iota((8, 128), 1), 4)
    for k in range(NZ):
        oz = lax.rem(z + k, NZ)
        m = (NZ - k) % NZ
        here_cf = (tile_row == m // 8) & (tile_group == m % 8)
        here_id = (tile_row == m // 8 + 2) & (tile_group == m % 8)
        tile = jnp.where(here_cf, vcf[pl.ds(oz, 1), :], 0.0)
        cz_send[k] = jnp.where(here_id, vid[pl.ds(oz, 1), :], tile)
    cz_recv[0] = cz_send[0]
    cz_copies = [go(cz_send.at[k], cz_recv.at[NZ - k], cz_s.at[k - 1], cz_r.at[NZ - k - 1], along(k), j) for k in FAR_FIRST]

    def leaf(i, side, part_ref, leaf_ref, ssem, rsem, log):
        k, n, to = (2 * i + 1, i, along(1)) if side == 0 else (15 - 2 * i, 4 + i, along(-1))
        log[n] = go(part_ref.at[k], leaf_ref.at[side, i], ssem.at[n], rsem.at[n], to, j)

    def chain(s, side, part_ref, leaf_ref, chain_ref, ssem, rsem, log):
        k = 8 - 2 * s if side == 0 else 8 + 2 * s
        n = 8 + 4 * side + s
        if s > (0 if side == 0 else 1):
            log[n - 1].wait_recv()
            part_ref[k] += chain_ref[side, s - 1]
        if s > 0:
            log[4 * side + 4 - s].wait_recv()
            part_ref[k] += leaf_ref[side, 4 - s]
        log[n] = go(part_ref.at[k], chain_ref.at[side, s], ssem.at[n], rsem.at[n], along(2 - 4 * side), j)

    sums = (zp_part, zp_leaf)
    ends = (pr_s, pr_r, {})

    def sums_stage(s):
        chain(s, 0, *sums, zp_chain, *ends)
        if s > 0:
            chain(s, 1, *sums, zp_chain, *ends)

    def leaves(i):
        leaf(i, 0, *sums, *ends)
        leaf(i, 1, *sums, *ends)

    def both_halves(k):
        at = slice(k * 6, k * 6 + 6)
        zp_part[k, 0:6, :] = p32[at, :] + yg32[at, :]

    zp_part[...] = jnp.zeros((NZ, 8, 1024), F32)
    p32[0:96, :] = passage_part(yl)
    p_half = pall[...]
    qx_copies = []
    for d in range(3):
        qx_send[d] = dot(w_all[xs[d]], p_half, 0, 0).astype(BF16)
        qx_copies.append(go(qx_send.at[d], qx_recv.at[d], qx_s.at[d], qx_r.at[d], xdp[d], j))
    yg_copies[0].wait_recv()
    yg32[16:80, :] = yg_recv[16:80, :].astype(F32)
    for k in range(4, 12):
        both_halves(k)
    leaves(3)
    sums_stage(0)
    leaves(2)

    mine_g = dot(w_all[x], p_half, 0, 0)
    for r in range(2):
        hi, lo = split(selt[r] * coef[r])
        rows_b = slots(pk_recv, r)
        mine_g = mine_g + dot(hi, rows_b, 0, 0) + dot(lo, rows_b, 0, 0)
    qg_ref[...] = mine_g
    sums_stage(1)
    for copy in yg_copies[1:]:
        copy.wait_recv()
    yg32[0:16, :] = yg_recv[0:16, :].astype(F32)
    yg32[80:96, :] = yg_recv[80:96, :].astype(F32)
    for k in (0, 1, 2, 3, 12, 13, 14, 15):
        both_halves(k)
    leaves(1)
    leaves(0)

    for copy in cz_copies + aq_copies:
        copy.wait_recv()
    tiles = cz_recv[0]
    for k in range(1, NZ):
        tiles = tiles + cz_recv[k]
    bank_sum = jnp.zeros((16, 1024), F32)
    bank_row = (iota((16, 128), 0) + 1).astype(F32)
    for h in range(2):
        hi, lo = split(jnp.where(tiles[h + 2 : h + 3] == bank_row, tiles[h : h + 1], 0.0))
        asked = aq_recv[8 * h : 8 * h + 8].reshape(128, 1024)
        bank_sum = bank_sum + dot(hi, asked, 1, 0) + dot(lo, asked, 1, 0)
    bg_ref[...] = SCALE * bank_sum
    sums_stage(2)
    for copy in qx_copies:
        copy.wait_recv()
    others = qx_recv[0].astype(F32) + qx_recv[1].astype(F32) + qx_recv[2].astype(F32)
    qg_ref[...] = SCALE * (qg_ref[...] + others)
    sums_stage(3)
    for n in (0, 4, 11, 15):
        ends[2][n].wait_recv()
    total_p = zp_part[0] + zp_leaf[0, 0] + zp_leaf[1, 0] + zp_chain[0, 3] + zp_chain[1, 3]
    pg_ref[...] = SCALE * total_p[0:6]
    for copy in sent:
        copy.wait_send()


def body(queries, passages, positive_bank, positive_ids, positive_counts):
    vmem = pl.BlockSpec(memory_space=pltpu.VMEM)
    hbm = pl.BlockSpec(memory_space=pl.ANY)
    dma = pltpu.SemaphoreType.DMA

    def buf(*shape):
        return pltpu.VMEM(shape, F32)

    def buf16(*shape):
        return pltpu.VMEM(shape, BF16)

    def sems(*counts):
        return [dma((n,)) for n in counts]

    scratch = [
        buf16(4, 128, 1024), buf16(NZ, 16, 1024), buf16(NZ, 2, 48, 128), buf(48, 128), buf(96, 128),
        buf(192, 1024), buf16(192, 1024),
        buf(2, 128, 128), buf(8, 128), buf(NC, 8, 128), buf16(256, 256), buf16(NC, 32, 1024),
        buf16(NC, 32, 1024), buf16(NC, 32, 1024), buf16(NC, 32, 1024),
        buf(4, 192, 128), buf(2, 192, 128), buf(192, 128), buf(192, 128), buf(4, 8, 128), buf(4, 8, 128),
        buf16(4, 192, 128), buf(4, 8, 128), buf(8, 128), buf(NC, 8, 128),
        buf16(96, 1024), buf16(96, 1024), buf(96, 1024), buf(NZ, 8, 1024), buf(2, 4, 8, 1024), buf(2, 4, 8, 1024),
        buf16(NZ, 16, 1024), buf16(NZ, 16, 1024), buf(16, 128), buf(16, 128), buf(NZ, 8, 128), buf(NZ, 8, 128),
        buf16(3, 128, 1024), buf16(3, 128, 1024),
        *sems(3, 3, 2, 16, 16, 16, 16, 7, 7, 7, 7, 7, 7, 7, 7),
        *sems(3, 3, 3, 3, 3, 3, 3, 3, 3, 3, 3, 3),
        *sems(15, 15, 15, 15, 16, 16, 3, 3, 2),
    ]
    losses, query_grad, passage_grad, bank_grad = pl.pallas_call(
        kernel,
        out_shape=(
            jax.ShapeDtypeStruct((1, 128), F32),
            jax.ShapeDtypeStruct((128, 1024), F32),
            jax.ShapeDtypeStruct((6, 1024), F32),
            jax.ShapeDtypeStruct((16, 1024), F32),
        ),
        in_specs=[hbm, vmem, hbm, vmem, vmem],
        out_specs=(vmem,) * 4,
        scratch_shapes=scratch,
        compiler_params=pltpu.CompilerParams(
            collective_id=0, has_side_effects=True, vmem_limit_bytes=48 * 2**20
        ),
    )(queries, passages, positive_bank, positive_ids.T, positive_counts.reshape(1, -1))
    return losses.reshape(-1), query_grad, passage_grad, bank_grad


def solution(mesh):
    placed = (P("dp", "sub"), P("dp", "sub"), P("dp", "sub"), P("dp", None), P("dp"))
    return jax.shard_map(
        body,
        mesh=mesh,
        in_specs=placed,
        out_specs=(P("dp"), P("dp", "sub"), P("dp", "sub"), P("dp", "sub")),
        check_vma=False,
    )
```

```python
import jax
import jax.numpy as jnp
from jax import lax
from jax.experimental import pallas as pl
from jax.experimental.pallas import tpu as pltpu
from jax.sharding import PartitionSpec as P

MESH = pl.DeviceIdType.MESH
F32 = jnp.float32
BF16 = jnp.bfloat16
NZ = 16
NC = 8
SCALE = 50.0
FAR_FIRST = (8, 7, 9, 6, 10, 5, 11, 4, 12, 3, 13, 2, 14, 1, 15)


def iota(shape, dim):
    return lax.broadcasted_iota(jnp.int32, shape, dim)


def dot(a, b, ca, cb):
    return lax.dot_general(a, b, (((ca,), (cb,)), ((), ())), preferred_element_type=F32)


def split(v):
    hi = v.astype(BF16)
    return hi, (v - hi.astype(F32)).astype(BF16)


def kernel(
    q_ref, p_ref, b_ref, ids_ref, cnt_ref,
    loss_ref, qg_ref, pg_ref, bg_ref,
    q4, bcol, pz, pb32, pz32, p32, pall,
    selt, idt, id_recv, smat, qs_send, qs_recv, pk_send, pk_recv,
    spart, sc1, sc2_send, sc2_recv, sl_send, sl_recv, ss_all, st_all, w_all, lt_all, cf, cf_recv,
    yg_send, yg_recv, yg32, zp_part, zp_leaf, zp_chain, aq_send, aq_recv, vid, vcf, cz_send, cz_recv, qx_send, qx_recv,
    q_s, q_r, pm_sem, bg_s, bg_r, pg_s, pg_r, sl_s, sl_r, qs_s, qs_r, id_s, id_r, pk_s, pk_r, cf_s, cf_r,
    sc_s, sc_r, ss_s, ss_r, st_s, st_r, w_s, w_r, lt_s, lt_r, yg_s, yg_r,
    aq_s, aq_r, cz_s, cz_r, pr_s, pr_r, qx_s, qx_r, in_sem,
):
    dp = lax.axis_index("dp")
    j = lax.axis_index("sub")
    z = lax.div(dp, NC)
    c = lax.rem(dp, NC)
    x = lax.div(c, 2)
    yl = lax.rem(c, 2)
    yh = lax.div(j, 2)
    core = lax.rem(j, 2)

    def along(d):
        return lax.rem(z + NZ + d, NZ) * NC + c

    mate = dp + 1 - 2 * yl
    plane_c = [lax.rem(c + d, NC) for d in range(1, NC)]
    plane = [z * NC + v for v in plane_c]
    xs = [lax.rem(x + d, 4) for d in range(1, 4)]
    xdp = [z * NC + v * 2 + yl for v in xs]
    subs = [j + 1 - 2 * core, j + 2 - 4 * yh, 3 - j]

    barrier = pltpu.get_barrier_semaphore()
    for to_dp in (along(1), along(-1), along(2), along(-2), *plane):
        pl.semaphore_signal(barrier, inc=1, device_id=(to_dp, j), device_id_type=MESH)
    for to_sub in subs:
        pl.semaphore_signal(barrier, inc=1, device_id=(dp, to_sub), device_id_type=MESH)

    sent = []

    def go(src, dst, ssem, rsem, to_dp, to_sub):
        copy = pltpu.make_async_remote_copy(
            src_ref=src, dst_ref=dst, send_sem=ssem, recv_sem=rsem,
            device_id=(to_dp, to_sub), device_id_type=MESH,
        )
        copy.start()
        sent.append(copy)
        return copy

    fetch_q = pltpu.make_async_copy(q_ref, q4.at[x], in_sem.at[0])
    fetch_b = pltpu.make_async_copy(b_ref, bcol.at[0], in_sem.at[1])
    fetch_q.start()
    fetch_b.start()

    p_own = p_ref[...].astype(F32)
    for k in range(8):
        pb32[k * 6 : k * 6 + 6, :] = p_own[:, k * 128 : (k + 1) * 128]
    pz[0, yl] = pb32[...].astype(BF16)

    row = iota((128, 128), 0)
    lane = iota((128, 128), 1)
    eye = lane == row

    def col_to_row(v):
        return jnp.sum(jnp.where(eye, v, 0.0), 0, keepdims=True)

    def row_to_col(v):
        return jnp.sum(jnp.where(eye, v, 0.0), 1, keepdims=True)

    ids = ids_ref[...]
    owner = lax.shift_right_arithmetic(ids, 4)
    place = jnp.where(
        ids >= 0, (owner & 7) * 16 + lax.shift_right_arithmetic(owner, 3), -1
    )
    local = (ids & 15).astype(F32)
    many = jnp.zeros((128, 128), F32)
    w_sum = jnp.zeros((128, 128), F32)
    w_max = jnp.full((128, 128), -1.0, F32)
    for k in range(16):
        hit = place[k : k + 1, :] == row
        w_k = local[k : k + 1, :]
        many = many + jnp.where(hit, 1.0, 0.0)
        w_sum = w_sum + jnp.where(hit, w_k, 0.0)
        w_max = jnp.maximum(w_max, jnp.where(hit, w_k, -1.0))
    earlier = jnp.where(row < lane, 1.0, 0.0).astype(BF16)
    before = dot(many.astype(BF16), earlier, 1, 0)
    twice = (many > 1.5) & (before < 0.5)
    first = (many > 0.5) & (before < 0.5)
    second = ((many > 0.5) & (before > 0.5)) | twice
    w_second = jnp.where(twice, w_sum - w_max, w_max)
    id0 = jnp.sum(jnp.where(first, w_max + 1.0, 0.0), 1, keepdims=True) - 1.0
    id1 = jnp.sum(jnp.where(second, w_second + 1.0, 0.0), 1, keepdims=True) - 1.0
    selt[0] = jnp.where(first, 1.0, 0.0)
    selt[1] = jnp.where(second, 1.0, 0.0)
    tile_row = iota((8, 128), 0)
    idt[...] = jnp.where(tile_row == 0, col_to_row(id0), col_to_row(id1))
    id_recv[c] = idt[...]
    fetch_q.wait()
    fetch_b.wait()
    for r in range(2):
        picked_q = dot(selt[r].astype(BF16), q4[x], 1, 0).astype(BF16)
        for k in range(NC):
            qs_send[k, r * 16 : (r + 1) * 16, :] = picked_q[k * 16 : (k + 1) * 16]
    qs_recv[c] = qs_send[c]

    pl.semaphore_wait(barrier, 14)

    def gather_stage(s, buf, ssem, rsem, log):
        if s > 0:
            log[s - 1][0].wait_recv()
            if s < 4:
                log[s - 1][3].wait_recv()
        if s == 4:
            return
        up = (NZ - 2 * s) % NZ
        got = [
            go(buf.at[up], buf.at[14 - 2 * s], ssem.at[4 * s], rsem.at[4 * s], along(2), j),
        ]
        far = None
        if s < 3:
            far = go(buf.at[2 * s], buf.at[2 * s + 2], ssem.at[4 * s + 3], rsem.at[4 * s + 3], along(-2), j)
        got += [
            go(buf.at[up], buf.at[15 - 2 * s], ssem.at[4 * s + 1], rsem.at[4 * s + 1], along(1), j),
            go(buf.at[2 * s], buf.at[2 * s + 1], ssem.at[4 * s + 2], rsem.at[4 * s + 2], along(-1), j),
            far,
        ]
        log.append(got)

    def sides(s, log):
        log[s][1].wait_recv()
        log[s][2].wait_recv()

    p_log, b_log = [], []
    pm_copy = go(pz.at[0, yl], pz.at[0, yl], pm_sem.at[0], pm_sem.at[1], mate, j)
    gather_stage(0, bcol, bg_s, bg_r, b_log)
    id_copies = [go(idt, id_recv.at[c], id_s.at[d], id_r.at[d], plane[d], j) for d in range(7)]
    q_copies = [go(q4.at[x], q4.at[x], q_s.at[d], q_r.at[d], xdp[d], j) for d in range(3)]
    pm_copy.wait_recv()
    gather_stage(0, pz, pg_s, pg_r, p_log)

    def spread(k):
        pz32[...] = pz[k].reshape(96, 128).astype(F32)
        for y in range(2):
            for b in range(8):
                at = y * 48 + b * 6
                to = y * 96 + k * 6
                p32[to : to + 6, b * 128 : (b + 1) * 128] = pz32[at : at + 6, :]

    spread(0)
    gather_stage(1, pz, pg_s, pg_r, p_log)
    gather_stage(1, bcol, bg_s, bg_r, b_log)
    sides(0, p_log)
    for k in (15, 14, 1, 2):
        spread(k)
    qs_copies = [go(qs_send.at[plane_c[d]], qs_recv.at[c], qs_s.at[d], qs_r.at[d], plane[d], j) for d in range(7)]
    gather_stage(2, pz, pg_s, pg_r, p_log)
    gather_stage(2, bcol, bg_s, bg_r, b_log)
    sides(1, p_log)
    for k in (13, 12, 3, 4):
        spread(k)

    for copy in id_copies:
        copy.wait_recv()
    mine = iota((16, 128), 1) == c * 16 + iota((16, 128), 0)

    def to_column(tile_rows):
        return jnp.sum(jnp.where(mine, tile_rows, 0.0), 1, keepdims=True)

    offset = iota((16, 256), 0) - z
    offset = jnp.where(offset < 0, offset + NZ, offset)
    bank_lane = (iota((16, 256), 1) - offset * 16).astype(F32)
    slot_lane = iota((16, 128), 1) & 15
    ids_by = jnp.zeros((16, 128), F32)
    for k in range(NC):
        for r in range(2):
            w_col = to_column(id_recv[k, r : r + 1, :])
            hot = (bank_lane == w_col) & (w_col > -0.5)
            at = k * 32 + r * 16
            smat[at : at + 16, :] = jnp.where(hot, 1.0, 0.0).astype(BF16)
            ids_by = jnp.where(slot_lane == k * 2 + r, w_col + 1.0, ids_by)
    vid[...] = ids_by

    gather_stage(3, pz, pg_s, pg_r, p_log)
    gather_stage(3, bcol, bg_s, bg_r, b_log)
    sides(2, p_log)
    for k in (11, 10, 5, 6):
        spread(k)
    gather_stage(4, pz, pg_s, pg_r, p_log)
    sides(3, p_log)
    for k in (9, 8, 7):
        spread(k)
    pall[...] = p32[...].astype(BF16)

    for copy in q_copies:
        copy.wait_recv()
    sc_copies = []
    for h in range(2):
        b = 1 - core + 2 * h
        spart[b] = dot(pall[...], q4[b], 1, 1)
        sc_copies.append(go(spart.at[b], sc1.at[h], sc_s.at[h], sc_r.at[h], dp, subs[0]))
    for h in range(2):
        b = core + 2 * h
        spart[b] = dot(pall[...], q4[b], 1, 1)

    for copy in sc_copies:
        copy.wait_recv()
    sc2_send[...] = spart[core + 2 - 2 * yh] + sc1[1 - yh]
    sc2_copy = go(sc2_send, sc2_recv, sc_s.at[2], sc_r.at[2], dp, subs[1])

    gather_stage(4, bcol, bg_s, bg_r, b_log)
    for n in range(4):
        sides(n, b_log)
    picked_b = dot(smat[...], bcol[...].reshape(256, 1024), 1, 0)
    pk_send[...] = picked_b.astype(BF16).reshape(NC, 32, 1024)
    for copy in qs_copies:
        copy.wait_recv()
    pair = jnp.sum(picked_b * qs_recv[...].reshape(256, 1024).astype(F32), 1, keepdims=True)
    for k in range(NC):
        two = []
        for r in range(2):
            at = k * 32 + r * 16
            two.append(jnp.sum(jnp.where(mine, pair[at : at + 16], 0.0), 0, keepdims=True))
        sl_send[k] = jnp.where(tile_row == 0, two[0], jnp.where(tile_row == 1, two[1], 0.0))
    sl_recv[c] = sl_send[c]
    sl_copies = [go(sl_send.at[plane_c[d]], sl_recv.at[c], sl_s.at[d], sl_r.at[d], plane[d], j) for d in range(7)]
    pk_copies = [go(pk_send.at[plane_c[d]], pk_recv.at[c], pk_s.at[d], pk_r.at[d], plane[d], j) for d in range(7)]
    pk_recv[c] = pk_send[c]

    goal = iota((256, 256), 0)
    plane_of = z + lax.shift_right_logical(goal, 4)
    plane_of = jnp.where(plane_of >= NZ, plane_of - NZ, plane_of)
    goal = (lax.shift_right_logical(goal, 1) & 7) * 32 + (goal & 1) * 16 + plane_of
    order = jnp.where(iota((256, 256), 1) == goal, 1.0, 0.0).astype(BF16)
    by_plane = dot(order, qs_recv[...].reshape(256, 1024), 1, 0)
    aq_send[...] = by_plane.astype(BF16).reshape(NZ, 16, 1024)
    aq_recv[0] = aq_send[0]
    aq_copies = [go(aq_send.at[k], aq_recv.at[NZ - k], aq_s.at[k - 1], aq_r.at[NZ - k - 1], along(k), j) for k in FAR_FIRST]

    for copy in sl_copies:
        copy.wait_recv()
    slot_tile = sl_recv[0]
    for k in range(1, NC):
        slot_tile = slot_tile + sl_recv[k]
    ss_all[j] = slot_tile
    ss_copies = [go(ss_all.at[j], ss_all.at[j], ss_s.at[d], ss_r.at[d], dp, subs[d]) for d in range(3)]
    inv_row = 1.0 / cnt_ref[...].astype(F32)
    has = [selt[r] > 0.5 for r in range(2)]
    live = [jnp.sum(selt[r], 1, keepdims=True) > 0.5 for r in range(2)]
    inv_slot = [jnp.sum(jnp.where(has[r], inv_row, 0.0), 1, keepdims=True) for r in range(2)]
    for copy in ss_copies:
        copy.wait_recv()
    ss_rows = (((ss_all[0] + ss_all[1]) + ss_all[2]) + ss_all[3]) * SCALE
    ss = [row_to_col(ss_rows[r : r + 1]) for r in range(2)]
    low = [jnp.where(has[r], ss[r], -jnp.inf) for r in range(2)]
    p_max = jnp.max(jnp.maximum(low[0], low[1]), 0, keepdims=True)
    p_exp = jnp.sum(jnp.exp(low[0] - p_max) + jnp.exp(low[1] - p_max), 0, keepdims=True)
    p_sum = jnp.sum(
        jnp.where(has[0], ss[0], 0.0) + jnp.where(has[1], ss[1], 0.0), 0, keepdims=True
    )

    sc2_copy.wait_recv()
    scores = (spart[j] + sc1[yh] + sc2_recv[...]) * SCALE
    m_own = jnp.max(scores, 0, keepdims=True)
    here = x == j
    p_top = jnp.where(here, p_max, m_own)
    p_tot = jnp.where(here, p_exp, 0.0)
    m_all = jnp.maximum(m_own, p_top)
    s_all = jnp.sum(jnp.exp(scores - m_all), 0, keepdims=True)
    s_all = s_all + p_tot * jnp.exp(p_top - m_all)
    st_all[x] = jnp.where(tile_row == 0, m_all, s_all)
    st_copies = [go(st_all.at[x], st_all.at[x], st_s.at[d], st_r.at[d], xdp[d], j) for d in range(3)]
    for copy in st_copies:
        copy.wait_recv()
    tops = [st_all[b, 0:1, :] for b in range(4)]
    m_top = jnp.maximum(jnp.maximum(tops[0], tops[1]), jnp.maximum(tops[2], tops[3]))
    total = st_all[0, 1:2, :] * jnp.exp(tops[0] - m_top)
    for b in range(1, 4):
        total = total + st_all[b, 1:2, :] * jnp.exp(tops[b] - m_top)
    log_total = m_top + jnp.log(total)
    lt_all[j] = jnp.broadcast_to(log_total, (8, 128))
    w_all[j] = jnp.exp(scores - log_total).astype(BF16)
    w_far = go(w_all.at[j], w_all.at[j], w_s.at[1], w_r.at[1], dp, subs[1])
    w_near = go(w_all.at[j], w_all.at[j], w_s.at[0], w_r.at[0], dp, subs[0])
    lt_copies = [go(lt_all.at[j], lt_all.at[j], lt_s.at[d], lt_r.at[d], dp, subs[d]) for d in range(3)]

    w_far.wait_recv()
    far = core + 2 - 2 * yh
    w_pass = go(w_all.at[far], w_all.at[far], w_s.at[2], w_r.at[2], dp, subs[0])
    for copy in lt_copies:
        copy.wait_recv()
    lt_row = lt_all[x, 0:1, :]
    coef = []
    for r in range(2):
        lt_slot = jnp.sum(jnp.where(has[r], lt_row, 0.0), 1, keepdims=True)
        weight = jnp.exp(jnp.where(live[r], ss[r] - lt_slot, 0.0))
        coef.append(jnp.where(live[r], weight - inv_slot[r], 0.0))
    cf[...] = jnp.where(tile_row == 0, col_to_row(coef[0]), col_to_row(coef[1]))
    cf_copies = [go(cf, cf_recv.at[c], cf_s.at[d], cf_r.at[d], plane[d], j) for d in range(7)]
    cf_recv[c] = cf[...]
    loss_ref[...] = lt_row - p_sum * inv_row

    w_near.wait_recv()
    w_pass.wait_recv()

    def passage_part(y):
        at = pl.multiple_of(y * 96, 96)
        acc = dot(w_all[0, pl.ds(at, 96), :], q4[0], 1, 0)
        for b in range(1, 4):
            acc = acc + dot(w_all[b, pl.ds(at, 96), :], q4[b], 1, 0)
        return acc

    yg_send[...] = passage_part(1 - yl).astype(BF16)
    yg_copies = []
    for n, (at, size) in enumerate(((16, 64), (0, 16), (80, 16))):
        piece = pl.ds(at, size)
        yg_copies.append(go(yg_send.at[piece], yg_recv.at[piece], yg_s.at[n], yg_r.at[n], mate, j))

    for copy in cf_copies:
        copy.wait_recv()
    cf_by = jnp.zeros((16, 128), F32)
    for k in range(NC):
        for r in range(2):
            cf_by = jnp.where(slot_lane == k * 2 + r, to_column(cf_recv[k, r : r + 1, :]), cf_by)
    vcf[...] = cf_by
    tile_group = lax.shift_right_logical(iota((8, 128), 1), 4)
    for k in range(NZ):
        oz = lax.rem(z + k, NZ)
        m = (NZ - k) % NZ
        here_cf = (tile_row == m // 8) & (tile_group == m % 8)
        here_id = (tile_row == m // 8 + 2) & (tile_group == m % 8)
        tile = jnp.where(here_cf, vcf[pl.ds(oz, 1), :], 0.0)
        cz_send[k] = jnp.where(here_id, vid[pl.ds(oz, 1), :], tile)
    cz_recv[0] = cz_send[0]
    cz_copies = [go(cz_send.at[k], cz_recv.at[NZ - k], cz_s.at[k - 1], cz_r.at[NZ - k - 1], along(k), j) for k in FAR_FIRST]

    def leaf(i, side, part_ref, leaf_ref, ssem, rsem, log):
        k, n, to = (2 * i + 1, i, along(1)) if side == 0 else (15 - 2 * i, 4 + i, along(-1))
        log[n] = go(part_ref.at[k], leaf_ref.at[side, i], ssem.at[n], rsem.at[n], to, j)

    def chain(s, side, part_ref, leaf_ref, chain_ref, ssem, rsem, log):
        k = 8 - 2 * s if side == 0 else 8 + 2 * s
        n = 8 + 4 * side + s
        if s > (0 if side == 0 else 1):
            log[n - 1].wait_recv()
            part_ref[k] += chain_ref[side, s - 1]
        if s > 0:
            log[4 * side + 4 - s].wait_recv()
            part_ref[k] += leaf_ref[side, 4 - s]
        log[n] = go(part_ref.at[k], chain_ref.at[side, s], ssem.at[n], rsem.at[n], along(2 - 4 * side), j)

    sums = (zp_part, zp_leaf)
    ends = (pr_s, pr_r, {})

    def sums_stage(s):
        chain(s, 0, *sums, zp_chain, *ends)
        if s > 0:
            chain(s, 1, *sums, zp_chain, *ends)

    def leaves(i):
        leaf(i, 0, *sums, *ends)
        leaf(i, 1, *sums, *ends)

    def both_halves(k):
        at = slice(k * 6, k * 6 + 6)
        zp_part[k, 0:6, :] = p32[at, :] + yg32[at, :]

    zp_part[...] = jnp.zeros((NZ, 8, 1024), F32)
    p32[0:96, :] = passage_part(yl)
    p_half = pall[...]
    qx_copies = []
    for d in range(3):
        qx_send[d] = dot(w_all[xs[d]], p_half, 0, 0).astype(BF16)
        qx_copies.append(go(qx_send.at[d], qx_recv.at[d], qx_s.at[d], qx_r.at[d], xdp[d], j))
    yg_copies[0].wait_recv()
    yg32[16:80, :] = yg_recv[16:80, :].astype(F32)
    for k in range(4, 12):
        both_halves(k)
    leaves(3)
    sums_stage(0)
    leaves(2)

    for copy in pk_copies:
        copy.wait_recv()

    def slots(ref, r):
        return ref[:, r * 16 : (r + 1) * 16, :].reshape(128, 1024)

    mine_g = dot(w_all[x], p_half, 0, 0)
    for r in range(2):
        hi, lo = split(selt[r] * coef[r])
        rows_b = slots(pk_recv, r)
        mine_g = mine_g + dot(hi, rows_b, 0, 0) + dot(lo, rows_b, 0, 0)
    qg_ref[...] = mine_g
    sums_stage(1)
    for copy in yg_copies[1:]:
        copy.wait_recv()
    yg32[0:16, :] = yg_recv[0:16, :].astype(F32)
    yg32[80:96, :] = yg_recv[80:96, :].astype(F32)
    for k in (0, 1, 2, 3, 12, 13, 14, 15):
        both_halves(k)
    leaves(1)
    leaves(0)

    for copy in cz_copies + aq_copies:
        copy.wait_recv()
    tiles = cz_recv[0]
    for k in range(1, NZ):
        tiles = tiles + cz_recv[k]
    bank_sum = jnp.zeros((16, 1024), F32)
    bank_row = (iota((16, 128), 0) + 1).astype(F32)
    for h in range(2):
        hi, lo = split(jnp.where(tiles[h + 2 : h + 3] == bank_row, tiles[h : h + 1], 0.0))
        asked = aq_recv[8 * h : 8 * h + 8].reshape(128, 1024)
        bank_sum = bank_sum + dot(hi, asked, 1, 0) + dot(lo, asked, 1, 0)
    bg_ref[...] = SCALE * bank_sum
    sums_stage(2)
    for copy in qx_copies:
        copy.wait_recv()
    others = qx_recv[0].astype(F32) + qx_recv[1].astype(F32) + qx_recv[2].astype(F32)
    qg_ref[...] = SCALE * (qg_ref[...] + others)
    sums_stage(3)
    for n in (0, 4, 11, 15):
        ends[2][n].wait_recv()
    total_p = zp_part[0] + zp_leaf[0, 0] + zp_leaf[1, 0] + zp_chain[0, 3] + zp_chain[1, 3]
    pg_ref[...] = SCALE * total_p[0:6]
    for copy in sent:
        copy.wait_send()


def body(queries, passages, positive_bank, positive_ids, positive_counts):
    vmem = pl.BlockSpec(memory_space=pltpu.VMEM)
    hbm = pl.BlockSpec(memory_space=pl.ANY)
    dma = pltpu.SemaphoreType.DMA

    def buf(*shape):
        return pltpu.VMEM(shape, F32)

    def buf16(*shape):
        return pltpu.VMEM(shape, BF16)

    def sems(*counts):
        return [dma((n,)) for n in counts]

    scratch = [
        buf16(4, 128, 1024), buf16(NZ, 16, 1024), buf16(NZ, 2, 48, 128), buf(48, 128), buf(96, 128),
        buf(192, 1024), buf16(192, 1024),
        buf(2, 128, 128), buf(8, 128), buf(NC, 8, 128), buf16(256, 256), buf16(NC, 32, 1024),
        buf16(NC, 32, 1024), buf16(NC, 32, 1024), buf16(NC, 32, 1024),
        buf(4, 192, 128), buf(2, 192, 128), buf(192, 128), buf(192, 128), buf(NC, 8, 128), buf(NC, 8, 128), buf(4, 8, 128), buf(4, 8, 128),
        buf16(4, 192, 128), buf(4, 8, 128), buf(8, 128), buf(NC, 8, 128),
        buf16(96, 1024), buf16(96, 1024), buf(96, 1024), buf(NZ, 8, 1024), buf(2, 4, 8, 1024), buf(2, 4, 8, 1024),
        buf16(NZ, 16, 1024), buf16(NZ, 16, 1024), buf(16, 128), buf(16, 128), buf(NZ, 8, 128), buf(NZ, 8, 128),
        buf16(3, 128, 1024), buf16(3, 128, 1024),
        *sems(3, 3, 2, 16, 16, 16, 16, 7, 7, 7, 7, 7, 7, 7, 7, 7, 7),
        *sems(3, 3, 3, 3, 3, 3, 3, 3, 3, 3, 3, 3),
        *sems(15, 15, 15, 15, 16, 16, 3, 3, 2),
    ]
    losses, query_grad, passage_grad, bank_grad = pl.pallas_call(
        kernel,
        out_shape=(
            jax.ShapeDtypeStruct((1, 128), F32),
            jax.ShapeDtypeStruct((128, 1024), F32),
            jax.ShapeDtypeStruct((6, 1024), F32),
            jax.ShapeDtypeStruct((16, 1024), F32),
        ),
        in_specs=[hbm, vmem, hbm, vmem, vmem],
        out_specs=(vmem,) * 4,
        scratch_shapes=scratch,
        compiler_params=pltpu.CompilerParams(
            collective_id=0, has_side_effects=True, vmem_limit_bytes=48 * 2**20
        ),
    )(queries, passages, positive_bank, positive_ids.T, positive_counts.reshape(1, -1))
    return losses.reshape(-1), query_grad, passage_grad, bank_grad


def solution(mesh):
    placed = (P("dp", "sub"), P("dp", "sub"), P("dp", "sub"), P("dp", None), P("dp"))
    return jax.shard_map(
        body,
        mesh=mesh,
        in_specs=placed,
        out_specs=(P("dp"), P("dp", "sub"), P("dp", "sub"), P("dp", "sub")),
        check_vma=False,
    )
```
